256 devices in a mesh: dp: 64 (over y, z, core), tower: 2 (over x_hi), mp: 2 (over x_lo).
Axes of the slice: x: 4 (x_hi: 2, x_lo: 2; x = x_hi * 2 + x_lo), y: 4, z: 8, core: 2. Of those that a mesh axis runs over, the one named last changes fastest.
Arguments:
- inputs: bfloat16 [2, 16384, 1536], P('tower', 'dp'), may hold values from -6 to 6
- head_weight: bfloat16 [2, 1152, 1536], P('tower', None, 'mp'), may hold values from -0.15625 to 0.15625
- pair_index: int32 [16384], P('dp'), may hold values from 0 to 16383, as said below
Outputs:
- grad_head: float32 [2, 1152, 1536], P('tower', 'dp', 'mp')
- grad_in: bfloat16 [2, 16384, 1536], P('tower', 'dp', 'mp')
The draws below stay inside these ranges and needn't reach their ends.
Inputs may be any that keep to these rules, and one draw needn't show every extreme that they name: Each aligned block of 256 entries is a permutation of that block's own indices: image i matches text pair_index[i], which lies in the same block.
All inputs are finite; a program needn't handle non-finite values.
Results may differ from the reference program's by a relative error of at most 0.019.
Values may be sent and summed in bfloat16 or wider, within the bound.
A program may use at most 128 MiB of HBM per device.

```python
import jax
import jax.numpy as jnp
from jax import lax

D = 1536
E = 1152
TOK_DEV = 256
BATCH = 16384
N_DP = 64


def draw_pair_index(key, part):
    key = jax.random.fold_in(key, 7)
    block_total = BATCH // TOK_DEV
    block_ids = jnp.arange(block_total).astype(jnp.int32)
    block_keys = jax.vmap(lambda number: jax.random.fold_in(key, number))(block_ids)
    shuffled = jax.vmap(lambda sub_key: jax.random.permutation(sub_key, TOK_DEV))(block_keys)
    return (shuffled + block_ids[:, None] * TOK_DEV).reshape(-1).astype(jnp.int32)


def steps_of(own_key, dims, pieces, smallest, top_value):
    level = 1.0
    for dim, parts in pieces:
        steps = jax.random.uniform(jax.random.fold_in(jax.random.fold_in(own_key, 6), dim), (parts,), jnp.float32, smallest / len(pieces), top_value / len(pieces))
        level = level * jnp.repeat(jnp.exp(steps), dims[dim] // parts).reshape((-1,) + (1,) * (len(dims) - 1 - dim))
    return level


def noise(rng, shape, scale, reach, split=(), kind=jnp.bfloat16):
    result = scale * jax.random.normal(rng, shape, jnp.float32)
    if split:
        result = result * steps_of(rng, shape, split, -0.22, 0.18)
    return jnp.clip(result, -reach, reach).astype(kind)


def setup_inputs(seed: int = 0) -> dict:
    key_of = jax.random.split(jax.random.key(seed), 4)
    return {
        "inputs": noise(key_of[0], (2, BATCH, D), 1.0, 6.0, ((0, 2), (1, 64))),
        "head_weight": noise(key_of[1], (2, E, D), D ** -0.5, 0.15625, ((0, 2), (2, 2))),
        "pair_index": draw_pair_index(jax.random.fold_in(key_of[3], 71), 0),
    }


EPSILON = 1e-06
LOGIT_SCALE = 100.0
LOGIT_BIAS = -10.0
LOSS_SCALE = 16384.0
HIGH = lax.Precision.HIGHEST

def rounded(values):
    return lax.optimization_barrier(values.astype(jnp.bfloat16)).astype(jnp.float32)

def forward(pooled, weight):
    pooled32 = pooled.astype(jnp.float32)
    scale_rms = jnp.sqrt(lax.optimization_barrier(jnp.mean(pooled32 * pooled32, axis=-1, keepdims=True)) + EPSILON)
    normed = rounded(pooled32 / scale_rms)
    projected = jnp.dot(normed, weight.astype(jnp.float32).T, precision=HIGH)
    inverse = lax.rsqrt(lax.optimization_barrier(jnp.sum(projected * projected, axis=-1, keepdims=True)) + EPSILON)
    return (scale_rms, normed, inverse, projected * inverse)

def backward(weight, scale_rms, normed, inverse, unit, grad_unit):
    dproj = rounded((grad_unit - unit * lax.optimization_barrier(jnp.sum(unit * grad_unit, axis=-1, keepdims=True))) * inverse)
    grad_weight = jnp.dot(dproj.T, normed, precision=HIGH)
    dnormed = jnp.dot(dproj, weight.astype(jnp.float32), precision=HIGH)
    grad_pooled = dnormed / scale_rms
    return (grad_weight, grad_pooled.astype(jnp.bfloat16))

def reference(inputs, head_weight, pair_index):
    image_side = forward(inputs[0], head_weight[0])
    text_side = forward(inputs[1], head_weight[1])
    image_emb = rounded(image_side[3])
    text_emb = rounded(text_side[3])
    weight_pair = LOSS_SCALE * LOGIT_SCALE / BATCH
    column_ids = jnp.arange(BATCH).astype(jnp.int32)

    def visit(text_grad, block_pair):
        image_rows, image_pos = block_pair
        logits = LOGIT_SCALE * jnp.dot(image_rows, text_emb.T, precision=HIGH) + LOGIT_BIAS
        sign_grid = jnp.where(image_pos[:, None] == column_ids[None, :], 1.0, -1.0).astype(jnp.float32)
        coeffs = rounded(-weight_pair * sign_grid * jax.nn.sigmoid(-sign_grid * logits))
        text_next = text_grad + jnp.dot(coeffs.T, image_rows, precision=HIGH)
        return (text_next, jnp.dot(coeffs, text_emb, precision=HIGH))
    text_grad, image_grad = lax.scan(visit, jnp.zeros((BATCH, E), jnp.float32), (image_emb.reshape(N_DP, TOK_DEV, E), pair_index.reshape(N_DP, TOK_DEV)))
    image_grad = image_grad.reshape(BATCH, E)
    image_weight, image_in = backward(head_weight[0], *image_side, image_grad)
    text_weight, text_in = backward(head_weight[1], *text_side, text_grad)
    return (jnp.stack([image_weight, text_weight]), jnp.stack([image_in, text_in]))
```

```python
import jax
import jax.numpy as jnp
from jax import lax
from jax.experimental import pallas as pl
from jax.experimental.pallas import tpu as pltpu
from jax.sharding import PartitionSpec as P

EPSILON = 1e-06
LOGIT_SCALE = 100.0
LOGIT_BIAS = -10.0
BATCH = 16384
LOSS_SCALE = 16384.0
WEIGHT_PAIR = LOSS_SCALE * LOGIT_SCALE / BATCH
MAX_EXPONENT = 88.0
NX, NY, NZ = 4, 4, 8
ROWS = 256
OWN = 128
HALF = 64
QUARTER = 32
E = 1152
D = 1536
DH = 768
LANES = 384
EY = 288
F32 = jnp.float32
BF16 = jnp.bfloat16
MESH = pl.DeviceIdType.MESH
NT = (((1,), (1,)), ((), ()))
TN = (((0,), (0,)), ((), ()))


def dot(a, b, dims=(((1,), (0,)), ((), ()))):
    return lax.dot_general(a, b, dims, preferred_element_type=F32)


def kernel(
    pooled, weight, pairs, gw_out, gin_out,
    normed, rms_s, hsend, hrecv, proj, unit, inv_s, ebuf,
    img, txt, igrad, tgrad,
    sib_send, sib_recv, zsend, zrecv, yr1, yr2, xsend, xl_recv, xr_recv, ib_send, ib_recv,
    grad, dfull,
    local, c_send, c_recv, wy_send, wy_r1, wy_r2, wz_send, wz_recv, wc_send, wc_recv,
    h_sem, ix_sem, zr_sem, sb_sem, tx_sem, ty_sem, tf_sem,
    rsb_sem, rz_sem, ry1_sem, ry2_sem, rx_sem, rr_sem, ib_sem, dx_sem,
    c_sem, wy1_sem, wy2_sem, wz_sem, wc_sem,
):
    dp = lax.axis_index("dp")
    tower = lax.axis_index("tower")
    mp = lax.axis_index("mp")
    x = tower * 2 + mp
    y = dp // 16
    z = (dp // 2) % 8
    c = dp % 2

    def at(nx, ny, nz, nc):
        return {"dp": (ny * NZ + nz) * 2 + nc, "tower": nx // 2, "mp": nx % 2}

    xl = at(tower * 2 + 1 - mp, y, z, c)
    xr = at(3 - x, y, z, c)
    sib = at(x, y, z, 1 - c)
    yn = (at(x, (y + 1) % NY, z, c), at(x, (y + NY - 1) % NY, z, c))
    zs = [at(x, y, (z + d) % NZ, c) for d in range(NZ)]
    zn = (zs[1], zs[NZ - 1])
    is_home = x >= 2
    is_image = x < 2
    first = jnp.where(is_home, x - 2, 1 - x)
    second = 1 - first
    order = (first, second)

    peers = [xl, xr, sib, yn[0], yn[1]] + zs[1:]
    barrier = pltpu.get_barrier_semaphore()
    for peer in peers:
        pl.semaphore_signal(barrier, inc=1, device_id=peer, device_id_type=MESH)
    pl.semaphore_wait(barrier, len(peers))

    sent = []

    def copy(src, dst, sem, device):
        return pltpu.make_async_remote_copy(
            src_ref=src, dst_ref=dst, send_sem=sem.at[0], recv_sem=sem.at[1],
            device_id=device, device_id_type=MESH,
        )

    def send(src, dst, sem, device):
        step = copy(src, dst, sem, device)
        step.start()
        sent.append((None, step))

    def send_if(cond, src, dst, sem, device):
        step = copy(src, dst, sem, device)
        pl.when(cond)(step.start)
        sent.append((cond, step))

    def arrived(dst, sem):
        copy(dst, dst, sem, sib).wait_recv()

    def arrived_if(cond, dst, sem):
        pl.when(cond)(copy(dst, dst, sem, sib).wait_recv)

    full = pooled[0].astype(F32)
    rms = jnp.sqrt(jnp.mean(full * full, axis=-1, keepdims=True) + EPSILON)
    rms_s[...] = rms
    part = pooled[0, :, pl.ds(pl.multiple_of(mp * DH, DH), DH)].astype(F32)
    normed[...] = (part / rms).astype(BF16)
    theirs = pl.ds(pl.multiple_of((1 - mp) * OWN, OWN), OWN)
    mine = pl.ds(pl.multiple_of(mp * OWN, OWN), OWN)
    hsend[...] = dot(normed[theirs, :], weight[0], NT).astype(BF16).reshape(2, HALF, E)
    for j in (1, 0):
        send(hsend.at[j], hrecv.at[j], h_sem.at[j], xl)
    proj[...] = dot(normed[mine, :], weight[0], NT)

    def y_sends(a, j):
        xs = order[a]
        for way, slot in ((0, 3), (1, 1)):
            send(txt.at[0, xs, j], txt.at[slot, xs, j], ty_sem.at[a, j, way], yn[way])

    for j in (1, 0):
        arrived(hrecv.at[j], h_sem.at[j])
        rows = pl.ds(j * HALF, HALF)
        value = proj[rows, :] + hrecv[j].astype(F32)
        inverse = lax.rsqrt(jnp.sum(value * value, axis=-1, keepdims=True) + EPSILON)
        inv_s[rows, :] = inverse
        unit_j = value * inverse
        unit[rows, :] = unit_j
        embedded = unit_j.astype(BF16)

        @pl.when(is_home)
        def _():
            txt[0, first, j] = embedded

        @pl.when(is_image)
        def _():
            if j == 0:
                img[0, 0] = embedded.reshape(2, QUARTER, E)
            else:
                ebuf[...] = embedded.reshape(2, QUARTER, E)

        if j == 1:
            send_if(is_image, ebuf, img.at[0, 0], ix_sem, xr)
        send_if(is_home, txt.at[0, first, j], txt.at[0, first, j], tx_sem.at[j, 0], xr)

    def ring_sends(k):
        for way in (0, 1):
            slot = (NZ - k) % NZ if way == 0 else k
            for ch in (0, 1):
                if k == 3 and ch != way:
                    continue
                to = (slot - 1) % NZ if way == 0 else (slot + 1) % NZ
                send(img.at[slot, 0, ch], img.at[to, 0, ch], zr_sem.at[k, way, ch], zn[way])

    def ring_arrive(k):
        for ch in (0, 1):
            for way in (0, 1):
                if k == 4 and ch != way:
                    continue
                slot = (NZ - k) % NZ if way == 0 else k
                arrived(img.at[slot, 0, ch], zr_sem.at[k - 1, way, ch])
                if k < 4 and not (k == 3 and ch != way):
                    to = (slot - 1) % NZ if way == 0 else (slot + 1) % NZ
                    send(img.at[slot, 0, ch], img.at[to, 0, ch], zr_sem.at[k, way, ch], zn[way])
                send(img.at[slot, 0, ch], img.at[slot, 1, ch], sb_sem.at[slot, ch], sib)

    def own_image():
        ring_sends(0)
        for ch in (0, 1):
            send(img.at[0, 0, ch], img.at[0, 1, ch], sb_sem.at[0, ch], sib)

    for j in (1, 0):
        arrived_if(is_image, txt.at[0, first, j], tx_sem.at[j, 0])
        if j == 1:
            arrived_if(is_home, img.at[0, 0], ix_sem)
            own_image()
        send(txt.at[0, first, j], txt.at[0, first, j], tx_sem.at[j, 1], xl)
        y_sends(0, j)
    ring_arrive(1)
    for j in (1, 0):
        arrived(txt.at[0, second, j], tx_sem.at[j, 1])
        y_sends(1, j)
    ring_arrive(2)

    def y_forward(a):
        xs = order[a]
        for way, slot in ((0, 3), (1, 1)):
            for j in (1, 0):
                arrived(txt.at[slot, xs, j], ty_sem.at[a, j, way])
                if j == way:
                    send(txt.at[slot, xs, j], txt.at[2, xs, j], tf_sem.at[a, j], yn[way])

    y_forward(0)
    ring_arrive(3)
    y_forward(1)
    ring_arrive(4)
    for a in (0, 1):
        for j in (0, 1):
            arrived(txt.at[2, order[a], j], tf_sem.at[a, j])
    for slot in range(NZ):
        for ch in (0, 1):
            arrived(img.at[slot, 1, ch], sb_sem.at[slot, ch])

    source = jnp.where(is_image, x * OWN, (3 - x) * OWN + HALF)
    positions = pairs[pl.ds(pl.multiple_of(source, HALF), HALF), :] - dp * ROWS
    columns = lax.broadcasted_iota(jnp.int32, (HALF, ROWS), 1)
    igrad[...] = jnp.zeros_like(igrad)

    def visit(t, carry):
        images = img[...].reshape(NZ * OWN, E)
        texts = txt[t].reshape(ROWS, E)
        logits = LOGIT_SCALE * dot(images, texts, NT) + LOGIT_BIAS
        tail = WEIGHT_PAIR / (1.0 + jnp.exp(jnp.minimum(-logits[HALF:], MAX_EXPONENT)))
        match = jnp.logical_and(positions == columns, t == 0)
        sign = jnp.where(match, 1.0, -1.0)
        head = -WEIGHT_PAIR * sign / (1.0 + jnp.exp(jnp.minimum(sign * logits[:HALF], MAX_EXPONENT)))
        coeffs = jnp.concatenate([head, tail], axis=0).astype(BF16)
        igrad[...] += dot(coeffs, texts)
        tgrad[t] = dot(coeffs, images, TN).astype(BF16).reshape(2, 2, HALF, E)
        return carry

    lax.fori_loop(0, NY, visit, 0)

    for a in (1, 0):
        for way in (0, 1):
            send(tgrad.at[2, order[a], way], yr1.at[a, way], ry1_sem.at[a, way], yn[way])
    ahead = (4, 3, 5, 2, 6, 1, 7, 0)
    for slot in ahead:
        sib_send[slot] = igrad[pl.ds(slot * OWN + HALF, HALF), :].astype(BF16)
        send(sib_send.at[slot], sib_recv.at[slot], rsb_sem.at[slot], sib)
    for a in (1, 0):
        for way, slot in ((0, 1), (1, 3)):
            send(tgrad.at[slot, order[a], 1 - way], yr2.at[a, way, 1 - way], ry2_sem.at[a, way, 1 - way], yn[way])

    def z_send(way, far, ch):
        slot = far if way == 0 else NZ - far
        rows = pl.ds(slot * OWN + ch * QUARTER, QUARTER)
        value = igrad[rows, :] + sib_recv[slot, pl.ds(ch * QUARTER, QUARTER), :].astype(F32)
        if far < 3 or (far == 3 and ch == way):
            arrived(zrecv.at[way, far, ch], rz_sem.at[way, far, ch])
            value = value + zrecv[way, far, ch].astype(F32)
        zsend[way, far - 1, ch] = value.astype(BF16)
        send(zsend.at[way, far - 1, ch], zrecv.at[way, far - 1, ch], rz_sem.at[way, far - 1, ch], zn[way])

    def y_second(a):
        xs = order[a]
        for way, slot in ((0, 1), (1, 3)):
            arrived(yr1.at[a, way], ry1_sem.at[a, way])
            tgrad[slot, xs, way] = (tgrad[slot, xs, way].astype(F32) + yr1[a, way].astype(F32)).astype(BF16)
            send(tgrad.at[slot, xs, way], yr2.at[a, way, way], ry2_sem.at[a, way, way], yn[way])

    for slot in (4, 3, 5):
        arrived(sib_recv.at[slot], rsb_sem.at[slot])
    for way in (0, 1):
        z_send(way, 4, way)
    for way in (0, 1):
        z_send(way, 3, 1 - way)
    y_second(1)
    for slot in (2, 6, 1, 7, 0):
        arrived(sib_recv.at[slot], rsb_sem.at[slot])
    for way in (0, 1):
        z_send(way, 3, way)
    y_second(0)
    for far in (2, 1):
        for way in (0, 1):
            z_send(way, far, 1 - way)
        for way in (0, 1):
            z_send(way, far, way)

    def y_total(a, j):
        for way in (0, 1):
            arrived(yr2.at[a, way, j], ry2_sem.at[a, way, j])
        return tgrad[0, order[a], j].astype(F32) + yr2[a, 0, j].astype(F32) + yr2[a, 1, j].astype(F32)

    for j in (0, 1):
        xsend[1, j] = y_total(1, j).astype(BF16)
        send(xsend.at[1, j], xl_recv.at[j], rx_sem.at[j], xl)

    for ch in (0, 1):
        rows = pl.ds(ch * QUARTER, QUARTER)
        value = igrad[rows, :] + sib_recv[0, rows, :].astype(F32)
        for way in (0, 1):
            arrived(zrecv.at[way, 0, ch], rz_sem.at[way, 0, ch])
            value = value + zrecv[way, 0, ch].astype(F32)

        @pl.when(is_image)
        def _():
            grad[rows, :] = value

        @pl.when(is_home)
        def _():
            ib_send[ch] = value.astype(BF16)

        send_if(is_home, ib_send.at[ch], ib_recv.at[ch], ib_sem.at[ch], xr)

    for j in (0, 1):
        value = y_total(0, j)
        arrived(xl_recv.at[j], rx_sem.at[j])
        value = value + xl_recv[j].astype(F32)

        @pl.when(is_image)
        def _():
            xsend[0, j] = value.astype(BF16)

        send_if(is_image, xsend.at[0, j], xr_recv.at[j], rr_sem.at[j], xr)

        @pl.when(is_home)
        def _():
            grad[pl.ds(j * HALF, HALF), :] = value

    @pl.when(is_image)
    def _():
        for ch in (0, 1):
            arrived(ib_recv.at[ch], ib_sem.at[ch])
        grad[pl.ds(HALF, HALF), :] = ib_recv[...].astype(F32).reshape(HALF, E)

    @pl.when(is_home)
    def _():
        for j in (0, 1):
            arrived(xr_recv.at[j], rr_sem.at[j])
            rows = pl.ds(j * HALF, HALF)
            grad[rows, :] = grad[rows, :] + xr_recv[j].astype(F32)

    unit_v = unit[...]
    grad_v = grad[...]
    dproj = (grad_v - unit_v * jnp.sum(unit_v * grad_v, axis=-1, keepdims=True)) * inv_s[...]
    dfull[mp] = dproj.astype(BF16)
    send(dfull.at[mp], dfull.at[mp], dx_sem, xl)
    arrived(dfull.at[1 - mp], dx_sem)

    dproj_all = dfull[...].reshape(ROWS, E)
    local[...] = dot(dproj_all, normed[...], TN)

    theirs_l = pl.ds(pl.multiple_of((1 - c) * LANES, LANES), LANES)
    mine_l = pl.ds(pl.multiple_of(c * LANES, LANES), LANES)
    for r in (2, 1, 3, 0):
        rows = pl.ds(pl.multiple_of(((y + r) % NY) * EY, EY), EY)
        c_send[r] = local[rows, theirs_l].astype(BF16)
        send(c_send.at[r], c_recv.at[r], c_sem.at[r], sib)

    dnormed = dot(dproj_all, weight[0])
    gin_out[0] = (dnormed / rms_s[...]).astype(BF16)

    EH = EY // 2

    def w_part(r, h):
        rows = pl.ds(pl.multiple_of(((y + r) % NY) * EY + h * EH, EH), EH)
        return local[rows, mine_l] + c_recv[r, pl.ds(h * EH, EH), :].astype(F32)

    arrived(c_recv.at[2], c_sem.at[2])
    for way in (0, 1):
        wy_send[way, 2] = w_part(2, way).astype(BF16)
        send(wy_send.at[way, 2], wy_r1.at[way], wy1_sem.at[way], yn[way])
    for way, r in ((0, 1), (1, 3)):
        arrived(c_recv.at[r], c_sem.at[r])
        wy_send[way, 1 - way] = w_part(r, 1 - way).astype(BF16)
        send(wy_send.at[way, 1 - way], wy_r2.at[way, 1 - way], wy2_sem.at[way, 1 - way], yn[way])
    for way, r in ((0, 1), (1, 3)):
        arrived(wy_r1.at[way], wy1_sem.at[way])
        wy_send[way, way] = (w_part(r, way) + wy_r1[way].astype(F32)).astype(BF16)
        send(wy_send.at[way, way], wy_r2.at[way, way], wy2_sem.at[way, way], yn[way])
    arrived(c_recv.at[0], c_sem.at[0])
    total = []
    for h in (0, 1):
        value = w_part(0, h)
        for way in (0, 1):
            arrived(wy_r2.at[way, h], wy2_sem.at[way, h])
            value = value + wy_r2[way, h].astype(F32)
        total.append(value.astype(BF16))
    total = jnp.concatenate(total, axis=0)
    out_row = lax.broadcasted_iota(jnp.int32, (NZ * 48, EY), 0)
    in_row = lax.broadcasted_iota(jnp.int32, (NZ * 48, EY), 1)
    group = out_row // 24
    inner = out_row - group * 24
    spread = jnp.where(jnp.logical_and(inner < 18, in_row == group * 18 + inner), 1.0, 0.0).astype(BF16)
    wz_send[...] = dot(spread, total).astype(BF16).reshape(NZ, 48, LANES)
    for d in range(1, NZ):
        send(wz_send.at[(z + d) % NZ], wz_recv.at[d], wz_sem.at[d], zs[d])
    value = wz_send[z].astype(F32)
    for d in range(1, NZ):
        arrived(wz_recv.at[d], wz_sem.at[d])
        value = value + wz_recv[d].astype(F32)
    wc_send[...] = value.reshape(2, 24, LANES)
    send(wc_send.at[1 - c], wc_recv, wc_sem, sib)
    gw_out[0, :, mine_l] = wc_send[c, :18, :]
    arrived(wc_recv, wc_sem)
    gw_out[0, :, theirs_l] = wc_recv[:18, :]

    for cond, step in sent:
        if cond is None:
            step.wait_send()
        else:
            pl.when(cond)(step.wait_send)


def scratch():
    vmem, dma = pltpu.VMEM, pltpu.SemaphoreType.DMA
    return [
        vmem((ROWS, DH), BF16), vmem((ROWS, 1), F32), vmem((2, HALF, E), BF16), vmem((2, HALF, E), BF16),
        vmem((OWN, E), F32), vmem((OWN, E), F32), vmem((OWN, 1), F32), vmem((2, QUARTER, E), BF16),
        vmem((NZ, 2, 2, QUARTER, E), BF16), vmem((NY, 2, 2, HALF, E), BF16),
        vmem((NZ * OWN, E), F32), vmem((NY, 2, 2, HALF, E), BF16),
        vmem((NZ, HALF, E), BF16), vmem((NZ, HALF, E), BF16),
        vmem((2, 4, 2, QUARTER, E), BF16), vmem((2, 4, 2, QUARTER, E), BF16),
        vmem((2, 2, HALF, E), BF16), vmem((2, 2, 2, HALF, E), BF16),
        vmem((2, 2, HALF, E), BF16), vmem((2, HALF, E), BF16), vmem((2, HALF, E), BF16),
        vmem((2, QUARTER, E), BF16), vmem((2, QUARTER, E), BF16),
        vmem((OWN, E), F32), vmem((2, OWN, E), BF16),
        vmem((E, DH), F32), vmem((NY, EY, LANES), BF16), vmem((NY, EY, LANES), BF16),
        vmem((2, 3, EY // 2, LANES), BF16), vmem((2, EY // 2, LANES), BF16), vmem((2, 2, EY // 2, LANES), BF16),
        vmem((NZ, 48, LANES), BF16), vmem((NZ, 48, LANES), BF16),
        vmem((2, 24, LANES), F32), vmem((24, LANES), F32),
        dma((2, 2)), dma((2,)), dma((4, 2, 2, 2)), dma((NZ, 2, 2)), dma((2, 2, 2)), dma((2, 2, 2, 2)),
        dma((2, 2, 2)),
        dma((NZ, 2)), dma((2, 4, 2, 2)), dma((2, 2, 2)), dma((2, 2, 2, 2)), dma((2, 2)), dma((2, 2)),
        dma((2, 2)), dma((2,)),
        dma((NY, 2)), dma((2, 2)), dma((2, 2, 2)), dma((NZ, 2)), dma((2,)),
    ]


def shards(inputs, head_weight, pair_index):
    space = pl.BlockSpec(memory_space=pltpu.VMEM)
    return pl.pallas_call(
        kernel,
        out_shape=(
            jax.ShapeDtypeStruct((1, E // 64, DH), F32),
            jax.ShapeDtypeStruct((1, ROWS, DH), BF16),
        ),
        in_specs=[space] * 3,
        out_specs=(space, space),
        scratch_shapes=scratch(),
        compiler_params=pltpu.CompilerParams(
            collective_id=0, has_side_effects=True, vmem_limit_bytes=60 * 2**20
        ),
    )(inputs, head_weight, pair_index.reshape(ROWS, 1))


def solution(mesh):
    in_specs = (P("tower", "dp", None), P("tower", None, "mp"), P("dp"))
    out_specs = (P("tower", "dp", "mp"), P("tower", "dp", "mp"))
    return jax.shard_map(shards, mesh=mesh, in_specs=in_specs, out_specs=out_specs, check_vma=False)
```

```python
import jax
import jax.numpy as jnp
from jax import lax
from jax.experimental import pallas as pl
from jax.experimental.pallas import tpu as pltpu
from jax.sharding import PartitionSpec as P

EPSILON = 1e-06
LOGIT_SCALE = 100.0
LOGIT_BIAS = -10.0
BATCH = 16384
LOSS_SCALE = 16384.0
WEIGHT_PAIR = LOSS_SCALE * LOGIT_SCALE / BATCH
LOG2E = 1.4426950408889634
MAX_POWER = 126.0
NX, NY, NZ = 4, 4, 8
ROWS = 256
OWN = 128
HALF = 64
QUARTER = 32
E = 1152
D = 1536
DH = 768
LANES = 128
POS = (0, 1, 3, 5, 7, 6, 4, 2)
EY = 288
F32 = jnp.float32
BF16 = jnp.bfloat16
MESH = pl.DeviceIdType.MESH
NT = (((1,), (1,)), ((), ()))
TN = (((0,), (0,)), ((), ()))


def dot(a, b, dims=(((1,), (0,)), ((), ()))):
    return lax.dot_general(a, b, dims, preferred_element_type=F32)


def kernel(
    pooled, weight, pairs, gw_out, gin_out,
    normed, rms_s, hsend, hrecv, proj, unit, inv_s, ebuf,
    img, txt, igrad, tgrad, tacc, town,
    sib_send, sib_recv, zsend, zrecv, yr1, yr2, xsend, xl_recv, xr_recv, ib_send, ib_recv,
    grad, dfull,
    local, c_send, c_recv, wy_send, wy_r1, wy_r2, wz_send, wz_recv, wc_send, wc_recv,
    h_sem, ix_sem, zr_sem, sb_sem, tx_sem, ty_sem, tf_sem,
    rsb_sem, rz_sem, ry1_sem, ry2_sem, rx_sem, rr_sem, ib_sem, dx_sem,
    c_sem, wy1_sem, wy2_sem, wz_sem, wc_sem,
):
    dp = lax.axis_index("dp")
    tower = lax.axis_index("tower")
    mp = lax.axis_index("mp")
    x = tower * 2 + mp
    y = dp // 16
    z = (dp // 2) % 8
    c = dp % 2

    def at(nx, ny, nz, nc):
        return {"dp": (ny * NZ + nz) * 2 + nc, "tower": nx // 2, "mp": nx % 2}

    xl = at(tower * 2 + 1 - mp, y, z, c)
    xr = at(3 - x, y, z, c)
    sib = at(x, y, z, 1 - c)
    yn = (at(x, (y + 1) % NY, z, c), at(x, (y + NY - 1) % NY, z, c))
    zs = [at(x, y, (z + d) % NZ, c) for d in range(NZ)]
    zn = (zs[1], zs[NZ - 1])
    is_home = x >= 2
    is_image = x < 2
    first = jnp.where(is_home, x - 2, 1 - x)
    second = 1 - first
    order = (first, second)

    peers = [xl, xr, sib, yn[0], yn[1]] + zs[1:]
    barrier = pltpu.get_barrier_semaphore()
    for peer in peers:
        pl.semaphore_signal(barrier, inc=1, device_id=peer, device_id_type=MESH)

    sent = []

    def copy(src, dst, sem, device):
        return pltpu.make_async_remote_copy(
            src_ref=src, dst_ref=dst, send_sem=sem.at[0], recv_sem=sem.at[1],
            device_id=device, device_id_type=MESH,
        )

    def send(src, dst, sem, device):
        step = copy(src, dst, sem, device)
        step.start()
        sent.append((None, step))

    def send_if(cond, src, dst, sem, device):
        step = copy(src, dst, sem, device)
        pl.when(cond)(step.start)
        sent.append((cond, step))

    def arrived(dst, sem):
        copy(dst, dst, sem, sib).wait_recv()

    full = pooled[0].astype(F32)
    rms = jnp.sqrt(jnp.mean(full * full, axis=-1, keepdims=True) + EPSILON)
    rms_s[...] = rms
    part = pooled[0, :, pl.ds(pl.multiple_of(mp * DH, DH), DH)].astype(F32)
    normed[...] = (part / rms).astype(BF16)
    theirs = pl.ds(pl.multiple_of((1 - mp) * OWN, OWN), OWN)
    mine = pl.ds(pl.multiple_of(mp * OWN, OWN), OWN)
    hsend[...] = dot(normed[theirs, :], weight[0], NT).astype(BF16).reshape(2, HALF, E)
    pl.semaphore_wait(barrier, len(peers))
    for j in (1, 0):
        send(hsend.at[j], hrecv.at[j], h_sem.at[j], xl)
    proj[...] = dot(normed[mine, :], weight[0], NT)

    def text_first(j):
        steps = [copy(txt.at[0, first, j], txt.at[0, first, j], tx_sem.at[j, 1], xl)]
        for way, slot in ((0, 3), (1, 1)):
            steps.append(copy(txt.at[0, first, j], txt.at[slot, first, j], ty_sem.at[0, j, way], yn[way]))
        return steps

    def own_image():
        for ch in (0, 1):
            for way in (0, 1):
                to = POS[NZ - 1] if way == 0 else POS[1]
                steps = copy(img.at[0, 0, ch], img.at[to, 0, ch], zr_sem.at[0, way, ch], zn[way])
                steps.start()
            copy(img.at[0, 0, ch], img.at[0, 1, ch], sb_sem.at[0, ch], sib).start()

    for j in (1, 0):
        arrived(hrecv.at[j], h_sem.at[j])
        rows = pl.ds(j * HALF, HALF)
        value = proj[rows, :] + hrecv[j].astype(F32)
        inverse = lax.rsqrt(jnp.sum(value * value, axis=-1, keepdims=True) + EPSILON)
        inv_s[rows, :] = inverse
        unit_j = value * inverse
        unit[rows, :] = unit_j
        embedded = unit_j.astype(BF16)

        @pl.when(is_home)
        def _():
            txt[0, first, j] = embedded
            copy(txt.at[0, first, j], txt.at[0, first, j], tx_sem.at[j, 0], xr).start()
            for step in text_first(j):
                step.start()

        @pl.when(is_image)
        def _():
            if j == 0:
                img[0, 0] = embedded.reshape(2, QUARTER, E)
                own_image()
            else:
                ebuf[...] = embedded.reshape(2, QUARTER, E)
                copy(ebuf, img.at[0, 0], ix_sem, xr).start()

        sent.append((is_home, copy(txt.at[0, first, j], txt.at[0, first, j], tx_sem.at[j, 0], xr)))
        sent.extend((None, step) for step in text_first(j))
    sent.append((is_image, copy(ebuf, img.at[0, 0], ix_sem, xr)))
    for ch in (0, 1):
        for way in (0, 1):
            to = POS[NZ - 1] if way == 0 else POS[1]
            sent.append((None, copy(img.at[0, 0, ch], img.at[to, 0, ch], zr_sem.at[0, way, ch], zn[way])))
        sent.append((None, copy(img.at[0, 0, ch], img.at[0, 1, ch], sb_sem.at[0, ch], sib)))

    @pl.when(is_home)
    def _():
        arrived(img.at[0, 0], ix_sem)
        own_image()

    @pl.when(is_image)
    def _():
        for j in (1, 0):
            arrived(txt.at[0, first, j], tx_sem.at[j, 0])
            for step in text_first(j):
                step.start()

    def ring_arrive(k):
        for ch in (0, 1):
            for way in (0, 1):
                if k == 4 and ch != way:
                    continue
                slot = (NZ - k) % NZ if way == 0 else k
                p = POS[slot]
                arrived(img.at[p, 0, ch], zr_sem.at[k - 1, way, ch])
                if k < 4 and not (k == 3 and ch != way):
                    to = POS[(slot - 1) % NZ if way == 0 else (slot + 1) % NZ]
                    send(img.at[p, 0, ch], img.at[to, 0, ch], zr_sem.at[k, way, ch], zn[way])
                send(img.at[p, 0, ch], img.at[p, 1, ch], sb_sem.at[p, ch], sib)

    def y_forward(a):
        xs = order[a]
        for way, slot in ((0, 3), (1, 1)):
            for j in (1, 0):
                arrived(txt.at[slot, xs, j], ty_sem.at[a, j, way])
                if j == way:
                    send(txt.at[slot, xs, j], txt.at[2, xs, j], tf_sem.at[a, j], yn[way])

    def sibling_images(low, high):
        for p in range(low, high):
            for ch in (0, 1):
                arrived(img.at[p, 1, ch], sb_sem.at[p, ch])

    mp_source = jnp.where(is_image, x, 3 - x)
    offset = jnp.where(is_image, 0, HALF)
    row = (pairs[pl.ds(mp_source, 1), :] - dp * ROWS).astype(F32)
    lane = lax.broadcasted_iota(jnp.int32, (HALF, OWN), 1)
    down = lax.broadcasted_iota(jnp.int32, (HALF, OWN), 0) + offset
    positions = jnp.sum(jnp.where(lane == down, row, 0.0), axis=1, keepdims=True)

    def block(t, low, high, masked=False):
        count = (high - low) * OWN
        images = img[low:high].reshape(count, E)
        texts = txt[t].reshape(ROWS, E)
        power = dot(images, texts, NT) * (-LOGIT_SCALE * LOG2E) - LOGIT_BIAS * LOG2E
        if masked:
            columns = lax.broadcasted_iota(jnp.int32, (HALF, ROWS), 1).astype(F32)
            sign = jnp.where(positions == columns, -1.0, 1.0)
            top = WEIGHT_PAIR * sign / (1.0 + jnp.exp2(jnp.minimum(sign * power[:HALF], MAX_POWER)))
            rest = WEIGHT_PAIR / (1.0 + jnp.exp2(jnp.minimum(power[HALF:], MAX_POWER)))
            coeffs = jnp.concatenate([top, rest], axis=0).astype(BF16)
        else:
            coeffs = (WEIGHT_PAIR / (1.0 + jnp.exp2(jnp.minimum(power, MAX_POWER)))).astype(BF16)
        rows = pl.ds(low * OWN, count)
        for_images = dot(coeffs, texts)
        if t == 0:
            igrad[rows, :] = for_images
        else:
            igrad[rows, :] += for_images
        return dot(coeffs, images, TN)

    ring_arrive(1)
    for j in (1, 0):
        arrived(txt.at[0, second, j], tx_sem.at[j, 1])
        for way, slot in ((0, 3), (1, 1)):
            send(txt.at[0, second, j], txt.at[slot, second, j], ty_sem.at[1, j, way], yn[way])
    sibling_images(0, 1)
    town[...] = block(0, 0, 1, masked=True)
    ring_arrive(2)
    y_forward(0)
    sibling_images(1, 3)
    town[...] += block(0, 1, 3)
    ring_arrive(3)
    sibling_images(3, 5)
    town[...] += block(0, 3, 5)
    y_forward(1)
    ring_arrive(4)
    sibling_images(5, 7)
    town[...] += block(0, 5, 7)
    sibling_images(7, 8)
    town[...] += block(0, 7, 8)

    for way, slot in ((0, 1), (1, 3)):
        tgrad[slot] = block(slot, 0, NZ).astype(BF16).reshape(2, 2, HALF, E)
        for a in (1, 0):
            send(tgrad.at[slot, order[a], 1 - way], yr2.at[a, way, 1 - way], ry2_sem.at[a, way, 1 - way], yn[way])

    for a in (0, 1):
        for j in (0, 1):
            arrived(txt.at[2, order[a], j], tf_sem.at[a, j])

    def sibling_rows(slot):
        p = POS[slot]
        sib_send[p] = igrad[pl.ds(p * OWN + HALF, HALF), :].astype(BF16)
        send(sib_send.at[p], sib_recv.at[p], rsb_sem.at[p], sib)

    def z_send(way, far, ch):
        slot = far if way == 0 else NZ - far
        p = POS[slot]
        rows = pl.ds(p * OWN + ch * QUARTER, QUARTER)
        value = igrad[rows, :] + sib_recv[p, pl.ds(ch * QUARTER, QUARTER), :].astype(F32)
        if far < 3 or (far == 3 and ch == way):
            arrived(zrecv.at[way, far, ch], rz_sem.at[way, far, ch])
            value = value + zrecv[way, far, ch].astype(F32)
        zsend[way, far - 1, ch] = value.astype(BF16)
        send(zsend.at[way, far - 1, ch], zrecv.at[way, far - 1, ch], rz_sem.at[way, far - 1, ch], zn[way])

    def sibling_here(*slots):
        for slot in slots:
            arrived(sib_recv.at[POS[slot]], rsb_sem.at[POS[slot]])

    tacc[...] = block(2, 7, 8)
    sibling_rows(4)
    tacc[...] += block(2, 5, 7)
    sibling_rows(3)
    sibling_rows(5)
    sibling_here(4)
    for way in (0, 1):
        z_send(way, 4, way)
    tacc[...] += block(2, 3, 5)
    sibling_rows(2)
    sibling_rows(6)
    sibling_here(3, 5)
    for way in (0, 1):
        z_send(way, 3, 1 - way)
    tacc[...] += block(2, 1, 3)
    sibling_rows(1)
    sibling_rows(7)
    tgrad[2] = (tacc[...] + block(2, 0, 1)).astype(BF16).reshape(2, 2, HALF, E)
    sibling_rows(0)

    for a in (1, 0):
        for way in (0, 1):
            send(tgrad.at[2, order[a], way], yr1.at[a, way], ry1_sem.at[a, way], yn[way])
    for way in (0, 1):
        z_send(way, 3, way)

    def y_second(a):
        xs = order[a]
        for way, slot in ((0, 1), (1, 3)):
            arrived(yr1.at[a, way], ry1_sem.at[a, way])
            tgrad[slot, xs, way] = (tgrad[slot, xs, way].astype(F32) + yr1[a, way].astype(F32)).astype(BF16)
            send(tgrad.at[slot, xs, way], yr2.at[a, way, way], ry2_sem.at[a, way, way], yn[way])

    sibling_here(2, 6, 1, 7, 0)
    for way in (0, 1):
        z_send(way, 2, 1 - way)
    y_second(1)
    for way in (0, 1):
        z_send(way, 2, way)
    y_second(0)
    for way in (0, 1):
        z_send(way, 1, 1 - way)
    for way in (0, 1):
        z_send(way, 1, way)

    def y_total(a, j):
        for way in (0, 1):
            arrived(yr2.at[a, way, j], ry2_sem.at[a, way, j])
        rows = pl.ds(pl.multiple_of(order[a] * OWN + j * HALF, HALF), HALF)
        return town[rows, :] + yr2[a, 0, j].astype(F32) + yr2[a, 1, j].astype(F32)

    for j in (0, 1):
        xsend[1, j] = y_total(1, j).astype(BF16)
        send(xsend.at[1, j], xl_recv.at[j], rx_sem.at[j], xl)

    for ch in (0, 1):
        rows = pl.ds(ch * QUARTER, QUARTER)
        value = igrad[rows, :] + sib_recv[0, rows, :].astype(F32)
        for way in (0, 1):
            arrived(zrecv.at[way, 0, ch], rz_sem.at[way, 0, ch])
            value = value + zrecv[way, 0, ch].astype(F32)

        @pl.when(is_image)
        def _():
            grad[rows, :] = value

        @pl.when(is_home)
        def _():
            ib_send[ch] = value.astype(BF16)

        send_if(is_home, ib_send.at[ch], ib_recv.at[ch], ib_sem.at[ch], xr)

    def dx_copy(j):
        part = pl.ds(j * HALF, HALF)
        return copy(dfull.at[mp, part], dfull.at[mp, part], dx_sem.at[j], xl)

    def backward(j):
        part = pl.ds(j * HALF, HALF)
        unit_v = unit[part, :]
        grad_v = grad[part, :]
        dproj = (grad_v - unit_v * jnp.sum(unit_v * grad_v, axis=-1, keepdims=True)) * inv_s[part, :]
        dfull[mp, part] = dproj.astype(BF16)
        dx_copy(j).start()

    pl.when(is_image)(lambda: backward(0))

    for j in (0, 1):
        value = y_total(0, j)
        arrived(xl_recv.at[j], rx_sem.at[j])
        value = value + xl_recv[j].astype(F32)

        @pl.when(is_image)
        def _():
            xsend[0, j] = value.astype(BF16)

        send_if(is_image, xsend.at[0, j], xr_recv.at[j], rr_sem.at[j], xr)

        @pl.when(is_home)
        def _():
            grad[pl.ds(j * HALF, HALF), :] = value

    @pl.when(is_image)
    def _():
        for ch in (0, 1):
            arrived(ib_recv.at[ch], ib_sem.at[ch])
        grad[pl.ds(HALF, HALF), :] = ib_recv[...].astype(F32).reshape(HALF, E)
        backward(1)

    @pl.when(is_home)
    def _():
        for j in (0, 1):
            arrived(xr_recv.at[j], rr_sem.at[j])
            rows = pl.ds(j * HALF, HALF)
            grad[rows, :] = grad[rows, :] + xr_recv[j].astype(F32)
            backward(j)

    for j in (0, 1):
        sent.append((None, dx_copy(j)))
    for j in (0, 1):
        part = pl.ds(j * HALF, HALF)
        arrived(dfull.at[1 - mp, part], dx_sem.at[j])
    dproj_all = dfull[...].reshape(ROWS, E)

    theirs_l = pl.ds(pl.multiple_of((1 - c) * LANES, LANES), LANES)
    mine_l = pl.ds(pl.multiple_of(c * LANES, LANES), LANES)
    for l in range(3):
        local[l] = dot(dproj_all, normed[:, l * 2 * LANES:(l + 1) * 2 * LANES], TN)
        c_send[l] = local[l, :, theirs_l].astype(BF16)
        send(c_send.at[l], c_recv.at[l], c_sem.at[l], sib)

    dnormed = dot(dproj_all, weight[0])
    gin_out[0] = (dnormed / rms_s[...]).astype(BF16)

    EH = EY // 2

    def w_part(l, r, h):
        rows = pl.ds(pl.multiple_of(((y + r) % NY) * EY + h * EH, EH), EH)
        return local[l, rows, mine_l] + c_recv[l, rows, :].astype(F32)

    for l in range(3):
        arrived(c_recv.at[l], c_sem.at[l])
        for way in (0, 1):
            wy_send[l, way, 2] = w_part(l, 2, way).astype(BF16)
            send(wy_send.at[l, way, 2], wy_r1.at[l, way], wy1_sem.at[l, way], yn[way])
        for way, r in ((0, 1), (1, 3)):
            wy_send[l, way, 1 - way] = w_part(l, r, 1 - way).astype(BF16)
            send(wy_send.at[l, way, 1 - way], wy_r2.at[l, way, 1 - way], wy2_sem.at[l, way, 1 - way], yn[way])
    for l in range(3):
        for way, r in ((0, 1), (1, 3)):
            arrived(wy_r1.at[l, way], wy1_sem.at[l, way])
            wy_send[l, way, way] = (w_part(l, r, way) + wy_r1[l, way].astype(F32)).astype(BF16)
            send(wy_send.at[l, way, way], wy_r2.at[l, way, way], wy2_sem.at[l, way, way], yn[way])
    out_row = lax.broadcasted_iota(jnp.int32, (NZ * 48, EY), 0)
    in_row = lax.broadcasted_iota(jnp.int32, (NZ * 48, EY), 1)
    group = out_row // 24
    inner = out_row - group * 24
    spread = jnp.where(jnp.logical_and(inner < 18, in_row == group * 18 + inner), 1.0, 0.0).astype(BF16)
    for l in range(3):
        total = []
        for h in (0, 1):
            value = w_part(l, 0, h)
            for way in (0, 1):
                arrived(wy_r2.at[l, way, h], wy2_sem.at[l, way, h])
                value = value + wy_r2[l, way, h].astype(F32)
            total.append(value.astype(BF16))
        total = jnp.concatenate(total, axis=0)
        wz_send[l] = dot(spread, total).astype(BF16).reshape(NZ, 48, LANES)
        for d in range(1, NZ):
            send(wz_send.at[l, (z + d) % NZ], wz_recv.at[l, d], wz_sem.at[l, d], zs[d])
    for l in range(3):
        value = wz_send[l, z].astype(F32)
        for d in range(1, NZ):
            arrived(wz_recv.at[l, d], wz_sem.at[l, d])
            value = value + wz_recv[l, d].astype(F32)
        wc_send[l] = value.reshape(2, 24, LANES)
        send(wc_send.at[l, 1 - c], wc_recv.at[l], wc_sem.at[l], sib)
        gw_out[0, :, pl.ds(pl.multiple_of((2 * l + c) * LANES, LANES), LANES)] = wc_send[l, c, :18, :]
    for l in range(3):
        arrived(wc_recv.at[l], wc_sem.at[l])
        gw_out[0, :, pl.ds(pl.multiple_of((2 * l + 1 - c) * LANES, LANES), LANES)] = wc_recv[l, :18, :]

    for cond, step in sent:
        if cond is None:
            step.wait_send()
        else:
            pl.when(cond)(step.wait_send)


def scratch():
    vmem, dma = pltpu.VMEM, pltpu.SemaphoreType.DMA
    return [
        vmem((ROWS, DH), BF16), vmem((ROWS, 1), F32), vmem((2, HALF, E), BF16), vmem((2, HALF, E), BF16),
        vmem((OWN, E), F32), vmem((OWN, E), F32), vmem((OWN, 1), F32), vmem((2, QUARTER, E), BF16),
        vmem((NZ, 2, 2, QUARTER, E), BF16), vmem((NY, 2, 2, HALF, E), BF16),
        vmem((NZ * OWN, E), F32), vmem((NY, 2, 2, HALF, E), BF16), vmem((ROWS, E), F32), vmem((ROWS, E), F32),
        vmem((NZ, HALF, E), BF16), vmem((NZ, HALF, E), BF16),
        vmem((2, 4, 2, QUARTER, E), BF16), vmem((2, 4, 2, QUARTER, E), BF16),
        vmem((2, 2, HALF, E), BF16), vmem((2, 2, 2, HALF, E), BF16),
        vmem((2, 2, HALF, E), BF16), vmem((2, HALF, E), BF16), vmem((2, HALF, E), BF16),
        vmem((2, QUARTER, E), BF16), vmem((2, QUARTER, E), BF16),
        vmem((OWN, E), F32), vmem((2, OWN, E), BF16),
        vmem((3, E, 2 * LANES), F32), vmem((3, E, LANES), BF16), vmem((3, E, LANES), BF16),
        vmem((3, 2, 3, EY // 2, LANES), BF16), vmem((3, 2, EY // 2, LANES), BF16), vmem((3, 2, 2, EY // 2, LANES), BF16),
        vmem((3, NZ, 48, LANES), BF16), vmem((3, NZ, 48, LANES), BF16),
        vmem((3, 2, 24, LANES), F32), vmem((3, 24, LANES), F32),
        dma((2, 2)), dma((2,)), dma((4, 2, 2, 2)), dma((NZ, 2, 2)), dma((2, 2, 2)), dma((2, 2, 2, 2)),
        dma((2, 2, 2)),
        dma((NZ, 2)), dma((2, 4, 2, 2)), dma((2, 2, 2)), dma((2, 2, 2, 2)), dma((2, 2)), dma((2, 2)),
        dma((2, 2)), dma((2, 2)),
        dma((3, 2)), dma((3, 2, 2)), dma((3, 2, 2, 2)), dma((3, NZ, 2)), dma((3, 2)),
    ]


def shards(inputs, head_weight, pair_index):
    space = pl.BlockSpec(memory_space=pltpu.VMEM)
    return pl.pallas_call(
        kernel,
        out_shape=(
            jax.ShapeDtypeStruct((1, E // 64, DH), F32),
            jax.ShapeDtypeStruct((1, ROWS, DH), BF16),
        ),
        in_specs=[space] * 3,
        out_specs=(space, space),
        scratch_shapes=scratch(),
        compiler_params=pltpu.CompilerParams(
            collective_id=0, has_side_effects=True, vmem_limit_bytes=60 * 2**20
        ),
    )(inputs, head_weight, pair_index.reshape(2, OWN))


def solution(mesh):
    in_specs = (P("tower", "dp", None), P("tower", None, "mp"), P("dp"))
    out_specs = (P("tower", "dp", "mp"), P("tower", "dp", "mp"))
    return jax.shard_map(shards, mesh=mesh, in_specs=in_specs, out_specs=out_specs, check_vma=False)
```

```python
import jax
import jax.numpy as jnp
from jax import lax
from jax.experimental import pallas as pl
from jax.experimental.pallas import tpu as pltpu
from jax.sharding import PartitionSpec as P

EPSILON = 1e-06
LOGIT_SCALE = 100.0
LOGIT_BIAS = -10.0
BATCH = 16384
LOSS_SCALE = 16384.0
WEIGHT_PAIR = LOSS_SCALE * LOGIT_SCALE / BATCH
LOG2E = 1.4426950408889634
MAX_POWER = 126.0
NX, NY, NZ = 4, 4, 8
ROWS = 256
OWN = 128
HALF = 64
QUARTER = 32
E = 1152
D = 1536
DH = 768
LANES = 128
POS = (0, 1, 3, 5, 7, 6, 4, 2)
EY = 288
TURN = (2, 3, 0, 1)
RTURN = (0, 2, 1, 3)
F32 = jnp.float32
BF16 = jnp.bfloat16
MESH = pl.DeviceIdType.MESH
NT = (((1,), (1,)), ((), ()))
TN = (((0,), (0,)), ((), ()))


def dot(a, b, dims=(((1,), (0,)), ((), ()))):
    return lax.dot_general(a, b, dims, preferred_element_type=F32)


def kernel(
    pooled, weight, pairs, gw_out, gin_out,
    normed, rms_s, hsend, hrecv, proj, unit, inv_s, ebuf,
    img, txt, igrad, tgrad, coef, town, beside,
    sib_send, sib_recv, zsend, zrecv, yr1, yr2, xsend, xl_recv, xr_recv, ib_send, ib_recv,
    grad, dfull,
    local, c_send, c_recv, wy_send, wy_r1, wy_r2, wz_send, wz_recv, wc_send, wc_recv,
    h_sem, ix_sem, zr_sem, sb_sem, tx_sem, ty_sem, tf_sem,
    rsb_sem, rz_sem, ry1_sem, ry2_sem, rx_sem, rr_sem, ib_sem, dx_sem,
    c_sem, wy1_sem, wy2_sem, wz_sem, wc_sem,
):
    dp = lax.axis_index("dp")
    tower = lax.axis_index("tower")
    mp = lax.axis_index("mp")
    x = tower * 2 + mp
    y = dp // 16
    z = (dp // 2) % 8
    c = dp % 2

    def at(nx, ny, nz, nc):
        return {"dp": (ny * NZ + nz) * 2 + nc, "tower": nx // 2, "mp": nx % 2}

    xl = at(tower * 2 + 1 - mp, y, z, c)
    xr = at(3 - x, y, z, c)
    sib = at(x, y, z, 1 - c)
    yn = (at(x, (y + 1) % NY, z, c), at(x, (y + NY - 1) % NY, z, c))
    zs = [at(x, y, (z + d) % NZ, c) for d in range(NZ)]
    zn = (zs[1], zs[NZ - 1])
    is_home = x >= 2
    is_image = x < 2
    first = jnp.where(is_home, x - 2, 1 - x)
    second = 1 - first
    order = (first, second)

    peers = [xl, xr, sib, yn[0], yn[1]] + zs[1:]
    barrier = pltpu.get_barrier_semaphore()
    for peer in peers:
        pl.semaphore_signal(barrier, inc=1, device_id=peer, device_id_type=MESH)

    sent = []
    mode = {"run": True, "keep": True}

    def copy(src, dst, sem, device):
        return pltpu.make_async_remote_copy(
            src_ref=src, dst_ref=dst, send_sem=sem.at[0], recv_sem=sem.at[1],
            device_id=device, device_id_type=MESH,
        )

    def send(src, dst, sem, device, cond=None):
        step = copy(src, dst, sem, device)
        if mode["run"]:
            step.start()
        if mode["keep"]:
            sent.append((cond, step))

    def send_if(cond, src, dst, sem, device):
        step = copy(src, dst, sem, device)
        pl.when(cond)(step.start)
        sent.append((cond, step))

    def arrived(dst, sem):
        if mode["run"]:
            copy(dst, dst, sem, sib).wait_recv()

    def settle(count):
        for cond, step in sent[:count]:
            if cond is None:
                step.wait_send()
            else:
                pl.when(cond)(step.wait_send)
        del sent[:count]

    def only(cond, work):
        mode["keep"] = False
        pl.when(cond)(work)
        mode["keep"] = True

    def keep(work):
        mode["run"] = False
        work()
        mode["run"] = True

    full = pooled[0].astype(F32)
    rms = jnp.sqrt(jnp.mean(full * full, axis=-1, keepdims=True) + EPSILON)
    rms_s[...] = rms
    part = pooled[0, :, pl.ds(pl.multiple_of(mp * DH, DH), DH)].astype(F32)
    normed[...] = (part / rms).astype(BF16)
    theirs = pl.ds(pl.multiple_of((1 - mp) * OWN, OWN), OWN)
    mine = pl.ds(pl.multiple_of(mp * OWN, OWN), OWN)
    hsend[...] = dot(normed[theirs, :], weight[0], NT).astype(BF16).reshape(4, QUARTER, E)
    pl.semaphore_wait(barrier, len(peers))
    for j in TURN:
        send(hsend.at[j], hrecv.at[j], h_sem.at[j], xl)
    proj[...] = dot(normed[mine, :], weight[0], NT)

    def y_both(a, j):
        xs = order[a]
        for way, slot in ((0, 3), (1, 1)):
            send(txt.at[0, xs, j], txt.at[slot, xs, j], ty_sem.at[a, j, way], yn[way])

    def first_on(j):
        send(txt.at[0, first, j], txt.at[0, first, j], tx_sem.at[j, 1], xl)
        y_both(0, j)

    def own_image(ch):
        for way in (0, 1):
            to = POS[NZ - 1] if way == 0 else POS[1]
            send(img.at[0, 0, ch], img.at[to, 0, ch], zr_sem.at[0, way, ch], zn[way])
        send(img.at[0, 0, ch], img.at[0, 1, ch], sb_sem.at[0, ch], sib)

    for j in TURN:
        arrived(hrecv.at[j], h_sem.at[j])
        rows = pl.ds(j * QUARTER, QUARTER)
        value = proj[rows, :] + hrecv[j].astype(F32)
        inverse = lax.rsqrt(jnp.sum(value * value, axis=-1, keepdims=True) + EPSILON)
        inv_s[rows, :] = inverse
        unit_j = value * inverse
        unit[rows, :] = unit_j
        embedded = unit_j.astype(BF16)

        def text_start():
            send(txt.at[0, first, j], txt.at[0, first, j], tx_sem.at[j, 0], xr, is_home)
            first_on(j)

        def image_start():
            if j >= 2:
                send(ebuf.at[j - 2], img.at[0, 0, j - 2], ix_sem.at[j - 2], xr, is_image)
            else:
                own_image(j)

        def text_all():
            txt[0, first, j] = embedded
            text_start()

        def image_all():
            if j >= 2:
                ebuf[j - 2] = embedded
            else:
                img[0, 0, j] = embedded
            image_start()

        only(is_home, text_all)
        only(is_image, image_all)
        keep(text_start)
        keep(image_start)

    def ring(k, ch):
        for way in (0, 1):
            if k == 4 and ch != way:
                continue
            slot = (NZ - k) % NZ if way == 0 else k
            p = POS[slot]
            arrived(img.at[p, 0, ch], zr_sem.at[k - 1, way, ch])
            if k < 4 and not (k == 3 and ch != way):
                to = POS[(slot - 1) % NZ if way == 0 else (slot + 1) % NZ]
                send(img.at[p, 0, ch], img.at[to, 0, ch], zr_sem.at[k, way, ch], zn[way])
            send(img.at[p, 0, ch], img.at[p, 1, ch], sb_sem.at[p, ch], sib)

    def y_forward(a, j):
        xs = order[a]
        for way, slot in ((0, 3), (1, 1)):
            arrived(txt.at[slot, xs, j], ty_sem.at[a, j, way])
            if j // 2 == way:
                send(txt.at[slot, xs, j], txt.at[2, xs, j], tf_sem.at[a, j], yn[way])

    def first_here(j):
        arrived(txt.at[0, first, j], tx_sem.at[j, 0])
        first_on(j)

    def second_on(j):
        arrived(txt.at[0, second, j], tx_sem.at[j, 1])
        y_both(1, j)

    def image_device():
        first_here(2)
        first_here(3)
        first_here(0)
        ring(1, 0)
        first_here(1)
        ring(1, 1)
        second_on(2)
        second_on(3)
        ring(2, 0)
        second_on(0)
        ring(2, 1)
        y_forward(0, 0)
        second_on(1)
        y_forward(0, 2)
        y_forward(0, 3)
        y_forward(0, 1)

    def text_device():
        for ch in (0, 1):
            arrived(img.at[0, 0, ch], ix_sem.at[ch])
            own_image(ch)
        both_devices()

    def both_devices():
        y_forward(0, 2)
        y_forward(0, 3)
        second_on(2)
        second_on(3)
        y_forward(0, 0)
        second_on(0)
        ring(1, 0)
        y_forward(0, 1)
        second_on(1)
        ring(1, 1)
        ring(2, 0)
        ring(2, 1)

    only(is_image, image_device)
    only(is_home, text_device)
    keep(both_devices)

    def sibling_images(low, high):
        for p in range(low, high):
            for ch in (0, 1):
                arrived(img.at[p, 1, ch], sb_sem.at[p, ch])

    mp_source = jnp.where(is_image, x, 3 - x)
    offset = jnp.where(is_image, 0, HALF)
    row = (pairs[pl.ds(mp_source, 1), :] - dp * ROWS).astype(F32)
    lane = lax.broadcasted_iota(jnp.int32, (HALF, OWN), 1)
    down = lax.broadcasted_iota(jnp.int32, (HALF, OWN), 0) + offset
    positions = jnp.sum(jnp.where(lane == down, row, 0.0), axis=1, keepdims=True)

    def block(t, low, high, masked=False):
        count = (high - low) * OWN
        images = img[low:high].reshape(count, E)
        texts = txt[t].reshape(ROWS, E)
        power = dot(images, texts, NT) * (-LOGIT_SCALE * LOG2E) - LOGIT_BIAS * LOG2E
        if masked:
            columns = lax.broadcasted_iota(jnp.int32, (HALF, ROWS), 1).astype(F32)
            sign = jnp.where(positions == columns, -1.0, 1.0)
            top = WEIGHT_PAIR * sign / (1.0 + jnp.exp2(jnp.minimum(sign * power[:HALF], MAX_POWER)))
            rest = WEIGHT_PAIR / (1.0 + jnp.exp2(jnp.minimum(power[HALF:], MAX_POWER)))
            coeffs = jnp.concatenate([top, rest], axis=0).astype(BF16)
        else:
            coeffs = (WEIGHT_PAIR / (1.0 + jnp.exp2(jnp.minimum(power, MAX_POWER)))).astype(BF16)
        coef[pl.ds(low * OWN, count), t * ROWS:(t + 1) * ROWS] = coeffs
        return dot(coeffs, images, TN)

    def image_block(low, high):
        rows = pl.ds(low * OWN, (high - low) * OWN)
        igrad[rows, :] = dot(coef[rows, :], txt[...].reshape(NY * ROWS, E))

    y_forward(1, 2)
    ring(3, 0)
    y_forward(1, 3)
    ring(3, 1)
    y_forward(1, 0)
    y_forward(1, 1)
    sibling_images(0, 5)
    town[...] = block(0, 0, 5, masked=True)
    ring(4, 0)
    beside[0] = block(1, 0, 5)
    ring(4, 1)
    beside[1] = block(3, 0, 5)
    sibling_images(5, 8)

    gathered = len(sent)

    for way, slot in ((0, 1), (1, 3)):
        tgrad[slot] = (beside[way] + block(slot, 5, 8)).astype(BF16).reshape(2, 4, QUARTER, E)
        for a in (1, 0):
            for j in (2 - 2 * way, 3 - 2 * way):
                send(tgrad.at[slot, order[a], j], yr2.at[a, way, j], ry2_sem.at[a, way, j], yn[way])

    for a in (0, 1):
        for j in range(4):
            arrived(txt.at[2, order[a], j], tf_sem.at[a, j])

    def sibling_rows(slot):
        p = POS[slot]
        sib_send[p] = igrad[pl.ds(p * OWN + HALF, HALF), :].astype(BF16)
        send(sib_send.at[p], sib_recv.at[p], rsb_sem.at[p], sib)

    def z_send(way, far, ch):
        slot = far if way == 0 else NZ - far
        p = POS[slot]
        rows = pl.ds(p * OWN + ch * QUARTER, QUARTER)
        value = igrad[rows, :] + sib_recv[p, pl.ds(ch * QUARTER, QUARTER), :].astype(F32)
        if far < 3 or (far == 3 and ch == way):
            arrived(zrecv.at[way, far, ch], rz_sem.at[way, far, ch])
            value = value + zrecv[way, far, ch].astype(F32)
        zsend[way, far - 1, ch] = value.astype(BF16)
        send(zsend.at[way, far - 1, ch], zrecv.at[way, far - 1, ch], rz_sem.at[way, far - 1, ch], zn[way])

    def sibling_here(*slots):
        for slot in slots:
            arrived(sib_recv.at[POS[slot]], rsb_sem.at[POS[slot]])

    tgrad[2] = block(2, 0, NZ).astype(BF16).reshape(2, 4, QUARTER, E)
    for a in (1, 0):
        for i in (0, 1):
            for way in (0, 1):
                j = 2 * way + i
                send(tgrad.at[2, order[a], j], yr1.at[a, j], ry1_sem.at[a, j], yn[way])

    town[...] += block(0, 5, 8)
    image_block(5, 8)
    for slot in (4, 3, 5):
        sibling_rows(slot)
    image_block(3, 5)
    for slot in (2, 6):
        sibling_rows(slot)
    sibling_here(4, 3, 5)
    for way in (0, 1):
        z_send(way, 4, way)
    for way in (0, 1):
        z_send(way, 3, 1 - way)
    image_block(0, 3)
    for slot in (1, 7, 0):
        sibling_rows(slot)

    def y_second(a, i):
        xs = order[a]
        for way, slot in ((0, 1), (1, 3)):
            j = 2 * way + i
            arrived(yr1.at[a, j], ry1_sem.at[a, j])
            tgrad[slot, xs, j] = (tgrad[slot, xs, j].astype(F32) + yr1[a, j].astype(F32)).astype(BF16)
            send(tgrad.at[slot, xs, j], yr2.at[a, way, j], ry2_sem.at[a, way, j], yn[way])

    def z_next(far, other):
        for way in (0, 1):
            z_send(way, far, 1 - way if other else way)

    settle(gathered)
    z_next(3, False)
    y_second(1, 0)
    sibling_here(2, 6, 1, 7, 0)
    z_next(2, True)
    y_second(1, 1)
    z_next(2, False)
    y_second(0, 0)
    z_next(1, True)
    y_second(0, 1)

    def y_total(a, j):
        for way in (0, 1):
            arrived(yr2.at[a, way, j], ry2_sem.at[a, way, j])
        rows = pl.ds(pl.multiple_of(order[a] * OWN + j * QUARTER, QUARTER), QUARTER)
        return town[rows, :] + yr2[a, 0, j].astype(F32) + yr2[a, 1, j].astype(F32)

    def dx_copy(j):
        part = pl.ds(j * QUARTER, QUARTER)
        return copy(dfull.at[mp, part], dfull.at[mp, part], dx_sem.at[j], xl)

    def backward(j):
        part = pl.ds(j * QUARTER, QUARTER)
        unit_v = unit[part, :]
        grad_v = grad[part, :]
        dproj = (grad_v - unit_v * jnp.sum(unit_v * grad_v, axis=-1, keepdims=True)) * inv_s[part, :]
        dfull[mp, part] = dproj.astype(BF16)
        dx_copy(j).start()

    def second_sum(j):
        xsend[1, j] = y_total(1, j).astype(BF16)
        send(xsend.at[1, j], xl_recv.at[j], rx_sem.at[j], xl)

    def first_sum(j):
        value = y_total(0, j)
        arrived(xl_recv.at[j], rx_sem.at[j])
        return value + xl_recv[j].astype(F32)

    def image_sum(ch):
        rows = pl.ds(ch * QUARTER, QUARTER)
        value = igrad[rows, :] + sib_recv[0, rows, :].astype(F32)
        for way in (0, 1):
            arrived(zrecv.at[way, 0, ch], rz_sem.at[way, 0, ch])
            value = value + zrecv[way, 0, ch].astype(F32)
        return value

    def first_out(j):
        xsend[0, j] = first_sum(j).astype(BF16)
        send(xsend.at[0, j], xr_recv.at[j], rr_sem.at[j], xr, is_image)

    def image_out(ch):
        ib_send[ch] = image_sum(ch).astype(BF16)
        send(ib_send.at[ch], ib_recv.at[ch], ib_sem.at[ch], xr, is_home)

    second_sum(0)
    second_sum(2)
    z_next(1, False)
    second_sum(1)
    second_sum(3)

    def image_tail():
        first_out(0)
        first_out(2)
        for ch in (0, 1):
            grad[pl.ds(ch * QUARTER, QUARTER), :] = image_sum(ch)
            backward(ch)
        first_out(1)
        first_out(3)
        for ch in (0, 1):
            arrived(ib_recv.at[ch], ib_sem.at[ch])
            grad[pl.ds(HALF + ch * QUARTER, QUARTER), :] = ib_recv[ch].astype(F32)
            backward(2 + ch)

    def text_tail():
        grad[pl.ds(0, QUARTER), :] = first_sum(0)
        image_out(0)
        image_out(1)
        for j in (2, 1, 3):
            grad[pl.ds(j * QUARTER, QUARTER), :] = first_sum(j)
        for j in RTURN:
            arrived(xr_recv.at[j], rr_sem.at[j])
            rows = pl.ds(j * QUARTER, QUARTER)
            grad[rows, :] = grad[rows, :] + xr_recv[j].astype(F32)
            backward(j)

    only(is_image, image_tail)
    only(is_home, text_tail)
    for j in range(4):
        sent.append((is_image, copy(xsend.at[0, j], xr_recv.at[j], rr_sem.at[j], xr)))
    for ch in (0, 1):
        sent.append((is_home, copy(ib_send.at[ch], ib_recv.at[ch], ib_sem.at[ch], xr)))

    settle(len(sent) - 10)
    for j in range(4):
        sent.append((None, dx_copy(j)))
    for j in range(4):
        part = pl.ds(j * QUARTER, QUARTER)
        arrived(dfull.at[1 - mp, part], dx_sem.at[j])
    dproj_all = dfull[...].reshape(ROWS, E)

    theirs_l = pl.ds(pl.multiple_of((1 - c) * LANES, LANES), LANES)
    mine_l = pl.ds(pl.multiple_of(c * LANES, LANES), LANES)
    for l in range(3):
        local[l] = dot(dproj_all, normed[:, l * 2 * LANES:(l + 1) * 2 * LANES], TN)
        c_send[l] = local[l, :, theirs_l].astype(BF16)
        send(c_send.at[l], c_recv.at[l], c_sem.at[l], sib)

    dnormed = dot(dproj_all, weight[0])
    gin_out[0] = (dnormed / rms_s[...]).astype(BF16)

    settle(len(sent) - 3)
    EH = EY // 2

    def w_part(l, r, h):
        rows = pl.ds(pl.multiple_of(((y + r) % NY) * EY + h * EH, EH), EH)
        return local[l, rows, mine_l] + c_recv[l, rows, :].astype(F32)

    for l in range(3):
        arrived(c_recv.at[l], c_sem.at[l])
        for way in (0, 1):
            wy_send[l, way, 2] = w_part(l, 2, way).astype(BF16)
            send(wy_send.at[l, way, 2], wy_r1.at[l, way], wy1_sem.at[l, way], yn[way])
        for way, r in ((0, 1), (1, 3)):
            wy_send[l, way, 1 - way] = w_part(l, r, 1 - way).astype(BF16)
            send(wy_send.at[l, way, 1 - way], wy_r2.at[l, way, 1 - way], wy2_sem.at[l, way, 1 - way], yn[way])
    for l in range(3):
        for way, r in ((0, 1), (1, 3)):
            arrived(wy_r1.at[l, way], wy1_sem.at[l, way])
            wy_send[l, way, way] = (w_part(l, r, way) + wy_r1[l, way].astype(F32)).astype(BF16)
            send(wy_send.at[l, way, way], wy_r2.at[l, way, way], wy2_sem.at[l, way, way], yn[way])
    settle(len(sent) - 18)
    out_row = lax.broadcasted_iota(jnp.int32, (NZ * 48, EY), 0)
    in_row = lax.broadcasted_iota(jnp.int32, (NZ * 48, EY), 1)
    group = out_row // 24
    inner = out_row - group * 24
    spread = jnp.where(jnp.logical_and(inner < 18, in_row == group * 18 + inner), 1.0, 0.0).astype(BF16)
    for l in range(3):
        total = []
        for h in (0, 1):
            value = w_part(l, 0, h)
            for way in (0, 1):
                arrived(wy_r2.at[l, way, h], wy2_sem.at[l, way, h])
                value = value + wy_r2[l, way, h].astype(F32)
            total.append(value.astype(BF16))
        total = jnp.concatenate(total, axis=0)
        wz_send[l] = dot(spread, total).astype(BF16).reshape(NZ, 48, LANES)
        for d in range(1, NZ):
            send(wz_send.at[l, (z + d) % NZ], wz_recv.at[l, d], wz_sem.at[l, d], zs[d])
    settle(len(sent) - 21)
    for l in range(3):
        value = wz_send[l, z].astype(F32)
        for d in range(1, NZ):
            arrived(wz_recv.at[l, d], wz_sem.at[l, d])
            value = value + wz_recv[l, d].astype(F32)
        wc_send[l] = value.reshape(2, 24, LANES)
        send(wc_send.at[l, 1 - c], wc_recv.at[l], wc_sem.at[l], sib)
        gw_out[0, :, pl.ds(pl.multiple_of((2 * l + c) * LANES, LANES), LANES)] = wc_send[l, c, :18, :]
    for l in range(3):
        arrived(wc_recv.at[l], wc_sem.at[l])
        gw_out[0, :, pl.ds(pl.multiple_of((2 * l + 1 - c) * LANES, LANES), LANES)] = wc_recv[l, :18, :]

    settle(len(sent))


def scratch():
    vmem, dma = pltpu.VMEM, pltpu.SemaphoreType.DMA
    return [
        vmem((ROWS, DH), BF16), vmem((ROWS, 1), F32), vmem((4, QUARTER, E), BF16), vmem((4, QUARTER, E), BF16),
        vmem((OWN, E), F32), vmem((OWN, E), F32), vmem((OWN, 1), F32), vmem((2, QUARTER, E), BF16),
        vmem((NZ, 2, 2, QUARTER, E), BF16), vmem((NY, 2, 4, QUARTER, E), BF16),
        vmem((NZ * OWN, E), F32), vmem((NY, 2, 4, QUARTER, E), BF16), vmem((NZ * OWN, NY * ROWS), BF16), vmem((ROWS, E), F32), vmem((2, ROWS, E), F32),
        vmem((NZ, HALF, E), BF16), vmem((NZ, HALF, E), BF16),
        vmem((2, 4, 2, QUARTER, E), BF16), vmem((2, 4, 2, QUARTER, E), BF16),
        vmem((2, 4, QUARTER, E), BF16), vmem((2, 2, 4, QUARTER, E), BF16),
        vmem((2, 4, QUARTER, E), BF16), vmem((4, QUARTER, E), BF16), vmem((4, QUARTER, E), BF16),
        vmem((2, QUARTER, E), BF16), vmem((2, QUARTER, E), BF16),
        vmem((OWN, E), F32), vmem((2, OWN, E), BF16),
        vmem((3, E, 2 * LANES), F32), vmem((3, E, LANES), BF16), vmem((3, E, LANES), BF16),
        vmem((3, 2, 3, EY // 2, LANES), BF16), vmem((3, 2, EY // 2, LANES), BF16), vmem((3, 2, 2, EY // 2, LANES), BF16),
        vmem((3, NZ, 48, LANES), BF16), vmem((3, NZ, 48, LANES), BF16),
        vmem((3, 2, 24, LANES), F32), vmem((3, 24, LANES), F32),
        dma((4, 2)), dma((2, 2)), dma((4, 2, 2, 2)), dma((NZ, 2, 2)), dma((4, 2, 2)), dma((2, 4, 2, 2)),
        dma((2, 4, 2)),
        dma((NZ, 2)), dma((2, 4, 2, 2)), dma((2, 4, 2)), dma((2, 2, 4, 2)), dma((4, 2)), dma((4, 2)),
        dma((2, 2)), dma((4, 2)),
        dma((3, 2)), dma((3, 2, 2)), dma((3, 2, 2, 2)), dma((3, NZ, 2)), dma((3, 2)),
    ]


def shards(inputs, head_weight, pair_index):
    space = pl.BlockSpec(memory_space=pltpu.VMEM)
    return pl.pallas_call(
        kernel,
        out_shape=(
            jax.ShapeDtypeStruct((1, E // 64, DH), F32),
            jax.ShapeDtypeStruct((1, ROWS, DH), BF16),
        ),
        in_specs=[space] * 3,
        out_specs=(space, space),
        scratch_shapes=scratch(),
        compiler_params=pltpu.CompilerParams(
            collective_id=0, has_side_effects=True, vmem_limit_bytes=60 * 2**20
        ),
    )(inputs, head_weight, pair_index.reshape(2, OWN))


def solution(mesh):
    in_specs = (P("tower", "dp", None), P("tower", None, "mp"), P("dp"))
    out_specs = (P("tower", "dp", "mp"), P("tower", "dp", "mp"))
    return jax.shard_map(shards, mesh=mesh, in_specs=in_specs, out_specs=out_specs, check_vma=False)
```

```python
import jax
import jax.numpy as jnp
from jax import lax
from jax.experimental import pallas as pl
from jax.experimental.pallas import tpu as pltpu
from jax.sharding import PartitionSpec as P

EPSILON = 1e-06
LOGIT_SCALE = 100.0
LOGIT_BIAS = -10.0
BATCH = 16384
LOSS_SCALE = 16384.0
WEIGHT_PAIR = LOSS_SCALE * LOGIT_SCALE / BATCH
LOG2E = 1.4426950408889634
MAX_POWER = 126.0
NX, NY, NZ = 4, 4, 8
ROWS = 256
OWN = 128
HALF = 64
QUARTER = 32
E = 1152
D = 1536
DH = 768
LANES = 128
POS = (0, 1, 3, 5, 7, 6, 4, 2)
EY = 288
TURN = (2, 3, 0, 1)
RTURN = (0, 2, 1, 3)
F32 = jnp.float32
BF16 = jnp.bfloat16
MESH = pl.DeviceIdType.MESH
NT = (((1,), (1,)), ((), ()))
TN = (((0,), (0,)), ((), ()))


def dot(a, b, dims=(((1,), (0,)), ((), ()))):
    return lax.dot_general(a, b, dims, preferred_element_type=F32)


def kernel(
    pooled, weight, pairs, gw_out, gin_out,
    normed, rms_s, hsend, hrecv, proj, unit, inv_s, ebuf,
    img, txt, igrad, tgrad, coef, town, beside,
    sib_send, sib_recv, zsend, zrecv, two_recv, yr1, yr2, xsend, xl_recv, xr_recv, ib_send, ib_recv,
    grad, dfull,
    local, c_send, c_recv, wy_send, wy_r1, wy_r2, wz_send, wz_recv, wc_send, wc_recv,
    h_sem, ix_sem, zr_sem, sb_sem, tx_sem, ty_sem, tf_sem,
    rsb_sem, rz_sem, two_sem, ry1_sem, ry2_sem, rx_sem, rr_sem, ib_sem, dx_sem,
    c_sem, wy1_sem, wy2_sem, wz_sem, wc_sem,
):
    dp = lax.axis_index("dp")
    tower = lax.axis_index("tower")
    mp = lax.axis_index("mp")
    x = tower * 2 + mp
    y = dp // 16
    z = (dp // 2) % 8
    c = dp % 2

    def at(nx, ny, nz, nc):
        return {"dp": (ny * NZ + nz) * 2 + nc, "tower": nx // 2, "mp": nx % 2}

    xl = at(tower * 2 + 1 - mp, y, z, c)
    xr = at(3 - x, y, z, c)
    sib = at(x, y, z, 1 - c)
    yn = (at(x, (y + 1) % NY, z, c), at(x, (y + NY - 1) % NY, z, c))
    zs = [at(x, y, (z + d) % NZ, c) for d in range(NZ)]
    zn = (zs[1], zs[NZ - 1])
    is_home = x >= 2
    is_image = x < 2
    first = jnp.where(is_home, x - 2, 1 - x)
    second = 1 - first
    order = (first, second)

    peers = [xl, xr, sib, yn[0], yn[1]] + zs[1:]
    barrier = pltpu.get_barrier_semaphore()
    for peer in peers:
        pl.semaphore_signal(barrier, inc=1, device_id=peer, device_id_type=MESH)

    sent = []
    mode = {"run": True, "keep": True}

    def copy(src, dst, sem, device):
        return pltpu.make_async_remote_copy(
            src_ref=src, dst_ref=dst, send_sem=sem.at[0], recv_sem=sem.at[1],
            device_id=device, device_id_type=MESH,
        )

    def send(src, dst, sem, device, cond=None):
        step = copy(src, dst, sem, device)
        if mode["run"]:
            step.start()
        if mode["keep"]:
            sent.append((cond, step))

    def send_if(cond, src, dst, sem, device):
        step = copy(src, dst, sem, device)
        pl.when(cond)(step.start)
        sent.append((cond, step))

    def arrived(dst, sem):
        if mode["run"]:
            copy(dst, dst, sem, sib).wait_recv()

    def settle(count):
        for cond, step in sent[:count]:
            if cond is None:
                step.wait_send()
            else:
                pl.when(cond)(step.wait_send)
        del sent[:count]

    def only(cond, work):
        mode["keep"] = False
        pl.when(cond)(work)
        mode["keep"] = True

    def keep(work):
        mode["run"] = False
        work()
        mode["run"] = True

    full = pooled[0].astype(F32)
    rms = jnp.sqrt(jnp.mean(full * full, axis=-1, keepdims=True) + EPSILON)
    rms_s[...] = rms
    part = pooled[0, :, pl.ds(pl.multiple_of(mp * DH, DH), DH)].astype(F32)
    normed[...] = (part / rms).astype(BF16)
    theirs = pl.ds(pl.multiple_of((1 - mp) * OWN, OWN), OWN)
    mine = pl.ds(pl.multiple_of(mp * OWN, OWN), OWN)
    hsend[...] = dot(normed[theirs, :], weight[0], NT).astype(BF16).reshape(4, QUARTER, E)
    pl.semaphore_wait(barrier, len(peers))
    for j in TURN:
        send(hsend.at[j], hrecv.at[j], h_sem.at[j], xl)
    proj[...] = dot(normed[mine, :], weight[0], NT)

    def y_both(a, j):
        xs = order[a]
        for way, slot in ((0, 3), (1, 1)):
            send(txt.at[0, xs, j], txt.at[slot, xs, j], ty_sem.at[a, j, way], yn[way])

    def first_on(j):
        send(txt.at[0, first, j], txt.at[0, first, j], tx_sem.at[j, 1], xl)
        y_both(0, j)

    def own_image(ch):
        for way in (0, 1):
            to = POS[NZ - 1] if way == 0 else POS[1]
            send(img.at[0, 0, ch], img.at[to, 0, ch], zr_sem.at[0, way, ch], zn[way])
        send(img.at[0, 0, ch], img.at[0, 1, ch], sb_sem.at[0, ch], sib)

    for j in TURN:
        arrived(hrecv.at[j], h_sem.at[j])
        rows = pl.ds(j * QUARTER, QUARTER)
        value = proj[rows, :] + hrecv[j].astype(F32)
        inverse = lax.rsqrt(jnp.sum(value * value, axis=-1, keepdims=True) + EPSILON)
        inv_s[rows, :] = inverse
        unit_j = value * inverse
        unit[rows, :] = unit_j
        embedded = unit_j.astype(BF16)

        def text_start():
            send(txt.at[0, first, j], txt.at[0, first, j], tx_sem.at[j, 0], xr, is_home)
            first_on(j)

        def image_start():
            if j >= 2:
                send(ebuf.at[j - 2], img.at[0, 0, j - 2], ix_sem.at[j - 2], xr, is_image)
            else:
                own_image(j)

        def text_all():
            txt[0, first, j] = embedded
            text_start()

        def image_all():
            if j >= 2:
                ebuf[j - 2] = embedded
            else:
                img[0, 0, j] = embedded
            image_start()

        only(is_home, text_all)
        only(is_image, image_all)
        keep(text_start)
        keep(image_start)

    def ring(k, ch):
        for way in (0, 1):
            if k == 4 and ch != way:
                continue
            slot = (NZ - k) % NZ if way == 0 else k
            p = POS[slot]
            arrived(img.at[p, 0, ch], zr_sem.at[k - 1, way, ch])
            if k < 4 and not (k == 3 and ch != way):
                to = POS[(slot - 1) % NZ if way == 0 else (slot + 1) % NZ]
                send(img.at[p, 0, ch], img.at[to, 0, ch], zr_sem.at[k, way, ch], zn[way])
            send(img.at[p, 0, ch], img.at[p, 1, ch], sb_sem.at[p, ch], sib)

    def y_forward(a, j):
        xs = order[a]
        for way, slot in ((0, 3), (1, 1)):
            arrived(txt.at[slot, xs, j], ty_sem.at[a, j, way])
            if a == 0 and j // 2 == way:
                send(txt.at[slot, xs, j], txt.at[2, xs, j], tf_sem.at[0, j], yn[way])

    def two_away(j):
        arrived(txt.at[2, first, j], tf_sem.at[0, j])
        send(txt.at[2, first, j], txt.at[2, first, j], tf_sem.at[1, j], xl)

    def first_here(j):
        arrived(txt.at[0, first, j], tx_sem.at[j, 0])
        first_on(j)

    def second_on(j):
        arrived(txt.at[0, second, j], tx_sem.at[j, 1])
        y_both(1, j)

    def image_device():
        first_here(2)
        first_here(3)
        first_here(0)
        ring(1, 0)
        first_here(1)
        ring(1, 1)
        second_on(2)
        second_on(3)
        ring(2, 0)
        second_on(0)
        ring(2, 1)
        y_forward(0, 0)
        second_on(1)
        y_forward(0, 2)
        y_forward(0, 3)
        y_forward(0, 1)

    def text_device():
        for ch in (0, 1):
            arrived(img.at[0, 0, ch], ix_sem.at[ch])
            own_image(ch)
        both_devices()

    def both_devices():
        y_forward(0, 2)
        y_forward(0, 3)
        second_on(2)
        second_on(3)
        y_forward(0, 0)
        second_on(0)
        ring(1, 0)
        y_forward(0, 1)
        second_on(1)
        ring(1, 1)
        ring(2, 0)
        ring(2, 1)

    only(is_image, image_device)
    only(is_home, text_device)
    keep(both_devices)

    def sibling_images(low, high):
        for p in range(low, high):
            for ch in (0, 1):
                arrived(img.at[p, 1, ch], sb_sem.at[p, ch])

    mp_source = jnp.where(is_image, x, 3 - x)
    offset = jnp.where(is_image, 0, HALF)
    row = (pairs[pl.ds(mp_source, 1), :] - dp * ROWS).astype(F32)
    lane = lax.broadcasted_iota(jnp.int32, (HALF, OWN), 1)
    down = lax.broadcasted_iota(jnp.int32, (HALF, OWN), 0) + offset
    positions = jnp.sum(jnp.where(lane == down, row, 0.0), axis=1, keepdims=True)

    def block(t, low, high, masked=False):
        count = (high - low) * OWN
        images = img[low:high].reshape(count, E)
        texts = txt[t].reshape(ROWS, E)
        power = dot(images, texts, NT) * (-LOGIT_SCALE * LOG2E) - LOGIT_BIAS * LOG2E
        if masked:
            columns = lax.broadcasted_iota(jnp.int32, (HALF, ROWS), 1).astype(F32)
            sign = jnp.where(positions == columns, -1.0, 1.0)
            top = WEIGHT_PAIR * sign / (1.0 + jnp.exp2(jnp.minimum(sign * power[:HALF], MAX_POWER)))
            rest = WEIGHT_PAIR / (1.0 + jnp.exp2(jnp.minimum(power[HALF:], MAX_POWER)))
            coeffs = jnp.concatenate([top, rest], axis=0).astype(BF16)
        else:
            coeffs = (WEIGHT_PAIR / (1.0 + jnp.exp2(jnp.minimum(power, MAX_POWER)))).astype(BF16)
        coef[pl.ds(low * OWN, count), t * ROWS:(t + 1) * ROWS] = coeffs
        return dot(coeffs, images, TN)

    def image_block(low, high):
        rows = pl.ds(low * OWN, (high - low) * OWN)
        igrad[rows, :] = dot(coef[rows, :], txt[...].reshape(NY * ROWS, E))

    y_forward(1, 2)
    ring(3, 0)
    y_forward(1, 3)
    ring(3, 1)
    two_away(2)
    two_away(3)
    y_forward(1, 0)
    y_forward(1, 1)
    sibling_images(0, 5)
    town[...] = block(0, 0, 5, masked=True)
    two_away(0)
    ring(4, 0)
    two_away(1)
    beside[0] = block(1, 0, 5)
    ring(4, 1)
    beside[1] = block(3, 0, 5)
    sibling_images(5, 8)

    gathered = len(sent)

    for way, slot in ((0, 1), (1, 3)):
        tgrad[slot] = (beside[way] + block(slot, 5, 8)).astype(BF16).reshape(2, 4, QUARTER, E)
        for a, chunks in ((1, RTURN), (0, (2 - 2 * way, 3 - 2 * way))):
            for j in chunks:
                send(tgrad.at[slot, order[a], j], yr2.at[a, way, j], ry2_sem.at[a, way, j], yn[way])

    for j in range(4):
        arrived(txt.at[2, second, j], tf_sem.at[1, j])

    def sibling_rows(slot):
        p = POS[slot]
        sib_send[p] = igrad[pl.ds(p * OWN + HALF, HALF), :].astype(BF16)
        send(sib_send.at[p], sib_recv.at[p], rsb_sem.at[p], sib)

    def z_send(way, far, ch):
        slot = far if way == 0 else NZ - far
        p = POS[slot]
        rows = pl.ds(p * OWN + ch * QUARTER, QUARTER)
        value = igrad[rows, :] + sib_recv[p, pl.ds(ch * QUARTER, QUARTER), :].astype(F32)
        if far < 3 or (far == 3 and ch == way):
            arrived(zrecv.at[way, far, ch], rz_sem.at[way, far, ch])
            value = value + zrecv[way, far, ch].astype(F32)
        zsend[way, far - 1, ch] = value.astype(BF16)
        send(zsend.at[way, far - 1, ch], zrecv.at[way, far - 1, ch], rz_sem.at[way, far - 1, ch], zn[way])

    def sibling_here(*slots):
        for slot in slots:
            arrived(sib_recv.at[POS[slot]], rsb_sem.at[POS[slot]])

    tgrad[2] = block(2, 0, NZ).astype(BF16).reshape(2, 4, QUARTER, E)
    for j in RTURN:
        send(tgrad.at[2, second, j], two_recv.at[j], two_sem.at[j], xl)

    town[...] += block(0, 5, 8)
    image_block(5, 8)
    for slot in (4, 3, 5):
        sibling_rows(slot)
    image_block(3, 5)
    for slot in (2, 6):
        sibling_rows(slot)
    sibling_here(4, 3, 5)
    for way in (0, 1):
        z_send(way, 4, way)
    for way in (0, 1):
        z_send(way, 3, 1 - way)
    for j in RTURN:
        arrived(two_recv.at[j], two_sem.at[j])
        tgrad[2, first, j] = (tgrad[2, first, j].astype(F32) + two_recv[j].astype(F32)).astype(BF16)
        send(tgrad.at[2, first, j], yr1.at[j], ry1_sem.at[j], yn[j // 2])
    image_block(0, 3)
    for slot in (1, 7, 0):
        sibling_rows(slot)

    def y_second(i):
        for way, slot in ((0, 1), (1, 3)):
            j = 2 * way + i
            arrived(yr1.at[j], ry1_sem.at[j])
            tgrad[slot, first, j] = (tgrad[slot, first, j].astype(F32) + yr1[j].astype(F32)).astype(BF16)
            send(tgrad.at[slot, first, j], yr2.at[0, way, j], ry2_sem.at[0, way, j], yn[way])

    def z_next(far, other):
        for way in (0, 1):
            z_send(way, far, 1 - way if other else way)

    settle(gathered)
    def y_total(a, j):
        for way in (0, 1):
            arrived(yr2.at[a, way, j], ry2_sem.at[a, way, j])
        rows = pl.ds(pl.multiple_of(order[a] * OWN + j * QUARTER, QUARTER), QUARTER)
        return town[rows, :] + yr2[a, 0, j].astype(F32) + yr2[a, 1, j].astype(F32)

    def dx_copy(j):
        part = pl.ds(j * QUARTER, QUARTER)
        return copy(dfull.at[mp, part], dfull.at[mp, part], dx_sem.at[j], xl)

    def backward(j):
        part = pl.ds(j * QUARTER, QUARTER)
        unit_v = unit[part, :]
        grad_v = grad[part, :]
        dproj = (grad_v - unit_v * jnp.sum(unit_v * grad_v, axis=-1, keepdims=True)) * inv_s[part, :]
        dfull[mp, part] = dproj.astype(BF16)
        dx_copy(j).start()

    def second_sum(j):
        xsend[1, j] = y_total(1, j).astype(BF16)
        send(xsend.at[1, j], xl_recv.at[j], rx_sem.at[j], xl)

    def first_sum(j):
        value = y_total(0, j)
        arrived(xl_recv.at[j], rx_sem.at[j])
        return value + xl_recv[j].astype(F32)

    def image_sum(ch):
        rows = pl.ds(ch * QUARTER, QUARTER)
        value = igrad[rows, :] + sib_recv[0, rows, :].astype(F32)
        for way in (0, 1):
            arrived(zrecv.at[way, 0, ch], rz_sem.at[way, 0, ch])
            value = value + zrecv[way, 0, ch].astype(F32)
        return value

    def first_out(j):
        xsend[0, j] = first_sum(j).astype(BF16)
        send(xsend.at[0, j], xr_recv.at[j], rr_sem.at[j], xr, is_image)

    def image_out(ch):
        ib_send[ch] = image_sum(ch).astype(BF16)
        send(ib_send.at[ch], ib_recv.at[ch], ib_sem.at[ch], xr, is_home)

    z_next(3, False)
    second_sum(0)
    second_sum(2)
    sibling_here(2, 6, 1, 7, 0)
    z_next(2, True)
    second_sum(1)
    second_sum(3)
    y_second(0)
    z_next(2, False)
    y_second(1)
    z_next(1, True)
    z_next(1, False)

    def image_tail():
        first_out(0)
        first_out(2)
        for ch in (0, 1):
            grad[pl.ds(ch * QUARTER, QUARTER), :] = image_sum(ch)
            backward(ch)
        first_out(1)
        first_out(3)
        for ch in (0, 1):
            arrived(ib_recv.at[ch], ib_sem.at[ch])
            grad[pl.ds(HALF + ch * QUARTER, QUARTER), :] = ib_recv[ch].astype(F32)
            backward(2 + ch)

    def text_tail():
        grad[pl.ds(0, QUARTER), :] = first_sum(0)
        image_out(0)
        image_out(1)
        for j in (2, 1, 3):
            grad[pl.ds(j * QUARTER, QUARTER), :] = first_sum(j)
        for j in RTURN:
            arrived(xr_recv.at[j], rr_sem.at[j])
            rows = pl.ds(j * QUARTER, QUARTER)
            grad[rows, :] = grad[rows, :] + xr_recv[j].astype(F32)
            backward(j)

    only(is_image, image_tail)
    only(is_home, text_tail)
    for j in range(4):
        sent.append((is_image, copy(xsend.at[0, j], xr_recv.at[j], rr_sem.at[j], xr)))
    for ch in (0, 1):
        sent.append((is_home, copy(ib_send.at[ch], ib_recv.at[ch], ib_sem.at[ch], xr)))

    settle(len(sent) - 10)
    for j in range(4):
        sent.append((None, dx_copy(j)))
    for j in range(4):
        part = pl.ds(j * QUARTER, QUARTER)
        arrived(dfull.at[1 - mp, part], dx_sem.at[j])
    dproj_all = dfull[...].reshape(ROWS, E)

    theirs_l = pl.ds(pl.multiple_of((1 - c) * LANES, LANES), LANES)
    mine_l = pl.ds(pl.multiple_of(c * LANES, LANES), LANES)
    for l in range(3):
        local[l] = dot(dproj_all, normed[:, l * 2 * LANES:(l + 1) * 2 * LANES], TN)
        c_send[l] = local[l, :, theirs_l].astype(BF16)
        send(c_send.at[l], c_recv.at[l], c_sem.at[l], sib)

    dnormed = dot(dproj_all, weight[0])
    gin_out[0] = (dnormed / rms_s[...]).astype(BF16)

    settle(len(sent) - 3)
    EH = EY // 2

    def w_part(l, r, h):
        rows = pl.ds(pl.multiple_of(((y + r) % NY) * EY + h * EH, EH), EH)
        return local[l, rows, mine_l] + c_recv[l, rows, :].astype(F32)

    for l in range(3):
        arrived(c_recv.at[l], c_sem.at[l])
        for way in (0, 1):
            wy_send[l, way, 2] = w_part(l, 2, way).astype(BF16)
            send(wy_send.at[l, way, 2], wy_r1.at[l, way], wy1_sem.at[l, way], yn[way])
        for way, r in ((0, 1), (1, 3)):
            wy_send[l, way, 1 - way] = w_part(l, r, 1 - way).astype(BF16)
            send(wy_send.at[l, way, 1 - way], wy_r2.at[l, way, 1 - way], wy2_sem.at[l, way, 1 - way], yn[way])
    for l in range(3):
        for way, r in ((0, 1), (1, 3)):
            arrived(wy_r1.at[l, way], wy1_sem.at[l, way])
            wy_send[l, way, way] = (w_part(l, r, way) + wy_r1[l, way].astype(F32)).astype(BF16)
            send(wy_send.at[l, way, way], wy_r2.at[l, way, way], wy2_sem.at[l, way, way], yn[way])
    settle(len(sent) - 18)
    out_row = lax.broadcasted_iota(jnp.int32, (NZ * 48, EY), 0)
    in_row = lax.broadcasted_iota(jnp.int32, (NZ * 48, EY), 1)
    group = out_row // 24
    inner = out_row - group * 24
    spread = jnp.where(jnp.logical_and(inner < 18, in_row == group * 18 + inner), 1.0, 0.0).astype(BF16)
    for l in range(3):
        total = []
        for h in (0, 1):
            value = w_part(l, 0, h)
            for way in (0, 1):
                arrived(wy_r2.at[l, way, h], wy2_sem.at[l, way, h])
                value = value + wy_r2[l, way, h].astype(F32)
            total.append(value.astype(BF16))
        total = jnp.concatenate(total, axis=0)
        wz_send[l] = dot(spread, total).astype(BF16).reshape(NZ, 48, LANES)
        for d in (4, 3, 5, 2, 6, 1, 7):
            send(wz_send.at[l, (z + d) % NZ], wz_recv.at[l, d], wz_sem.at[l, d], zs[d])
    settle(len(sent) - 21)
    for l in range(3):
        value = wz_send[l, z].astype(F32)
        for d in range(1, NZ):
            arrived(wz_recv.at[l, d], wz_sem.at[l, d])
            value = value + wz_recv[l, d].astype(F32)
        wc_send[l] = value.reshape(2, 24, LANES)
        send(wc_send.at[l, 1 - c], wc_recv.at[l], wc_sem.at[l], sib)
        gw_out[0, :, pl.ds(pl.multiple_of((2 * l + c) * LANES, LANES), LANES)] = wc_send[l, c, :18, :]
    for l in range(3):
        arrived(wc_recv.at[l], wc_sem.at[l])
        gw_out[0, :, pl.ds(pl.multiple_of((2 * l + 1 - c) * LANES, LANES), LANES)] = wc_recv[l, :18, :]

    settle(len(sent))


def finish(head, pooled, head_out, pooled_out):
    head_out[:, 0, :] = head[0]
    pooled_out[...] = pooled[...]


def scratch():
    vmem, dma = pltpu.VMEM, pltpu.SemaphoreType.DMA
    return [
        vmem((ROWS, DH), BF16), vmem((ROWS, 1), F32), vmem((4, QUARTER, E), BF16), vmem((4, QUARTER, E), BF16),
        vmem((OWN, E), F32), vmem((OWN, E), F32), vmem((OWN, 1), F32), vmem((2, QUARTER, E), BF16),
        vmem((NZ, 2, 2, QUARTER, E), BF16), vmem((NY, 2, 4, QUARTER, E), BF16),
        vmem((NZ * OWN, E), F32), vmem((NY, 2, 4, QUARTER, E), BF16), vmem((NZ * OWN, NY * ROWS), BF16), vmem((ROWS, E), F32), vmem((2, ROWS, E), F32),
        vmem((NZ, HALF, E), BF16), vmem((NZ, HALF, E), BF16),
        vmem((2, 4, 2, QUARTER, E), BF16), vmem((2, 4, 2, QUARTER, E), BF16),
        vmem((4, QUARTER, E), BF16), vmem((4, QUARTER, E), BF16), vmem((2, 2, 4, QUARTER, E), BF16),
        vmem((2, 4, QUARTER, E), BF16), vmem((4, QUARTER, E), BF16), vmem((4, QUARTER, E), BF16),
        vmem((2, QUARTER, E), BF16), vmem((2, QUARTER, E), BF16),
        vmem((OWN, E), F32), vmem((2, OWN, E), BF16),
        vmem((3, E, 2 * LANES), F32), vmem((3, E, LANES), BF16), vmem((3, E, LANES), BF16),
        vmem((3, 2, 3, EY // 2, LANES), BF16), vmem((3, 2, EY // 2, LANES), BF16), vmem((3, 2, 2, EY // 2, LANES), BF16),
        vmem((3, NZ, 48, LANES), BF16), vmem((3, NZ, 48, LANES), BF16),
        vmem((3, 2, 24, LANES), F32), vmem((3, 24, LANES), F32),
        dma((4, 2)), dma((2, 2)), dma((4, 2, 2, 2)), dma((NZ, 2, 2)), dma((4, 2, 2)), dma((2, 4, 2, 2)),
        dma((2, 4, 2)),
        dma((NZ, 2)), dma((2, 4, 2, 2)), dma((4, 2)), dma((4, 2)), dma((2, 2, 4, 2)), dma((4, 2)), dma((4, 2)),
        dma((2, 2)), dma((4, 2)),
        dma((3, 2)), dma((3, 2, 2)), dma((3, 2, 2, 2)), dma((3, NZ, 2)), dma((3, 2)),
    ]


def shards(inputs, head_weight, pair_index):
    space = pl.BlockSpec(memory_space=pltpu.VMEM)
    grads = pl.pallas_call(
        kernel,
        out_shape=(
            jax.ShapeDtypeStruct((1, E // 64, DH), F32),
            jax.ShapeDtypeStruct((1, ROWS, DH), BF16),
        ),
        in_specs=[space] * 3,
        out_specs=(space, space),
        scratch_shapes=scratch(),
        compiler_params=pltpu.CompilerParams(
            collective_id=0, has_side_effects=True, vmem_limit_bytes=60 * 2**20
        ),
    )(inputs, head_weight, pair_index.reshape(2, OWN))
    head, pooled = pl.pallas_call(
        finish,
        out_shape=(
            jax.ShapeDtypeStruct((E // 64, 1, DH), F32),
            jax.ShapeDtypeStruct((1, ROWS, DH), BF16),
        ),
        in_specs=[space] * 2,
        out_specs=(space, space),
    )(*grads)
    return head.reshape(1, E // 64, DH), pooled


def solution(mesh):
    in_specs = (P("tower", "dp", None), P("tower", None, "mp"), P("dp"))
    out_specs = (P("tower", "dp", "mp"), P("tower", "dp", "mp"))
    return jax.shard_map(shards, mesh=mesh, in_specs=in_specs, out_specs=out_specs, check_vma=False)
```

```python
import jax
import jax.numpy as jnp
from jax import lax
from jax.experimental import pallas as pl
from jax.experimental.pallas import tpu as pltpu
from jax.sharding import PartitionSpec as P

EPSILON = 1e-06
LOGIT_SCALE = 100.0
LOGIT_BIAS = -10.0
BATCH = 16384
LOSS_SCALE = 16384.0
WEIGHT_PAIR = LOSS_SCALE * LOGIT_SCALE / BATCH
LOG2E = 1.4426950408889634
MAX_POWER = 126.0
NX, NY, NZ = 4, 4, 8
ROWS = 256
OWN = 128
HALF = 64
QUARTER = 32
E = 1152
D = 1536
DH = 768
LANES = 128
POS = (0, 1, 3, 5, 7, 6, 4, 2)
EY = 288
TURN = (2, 3, 0, 1)
RTURN = (0, 2, 1, 3)
F32 = jnp.float32
BF16 = jnp.bfloat16
MESH = pl.DeviceIdType.MESH
NT = (((1,), (1,)), ((), ()))
TN = (((0,), (0,)), ((), ()))


def dot(a, b, dims=(((1,), (0,)), ((), ()))):
    return lax.dot_general(a, b, dims, preferred_element_type=F32)


def kernel(
    pooled_in, weight_in, pairs, gw_out, gin_out,
    pooled, weight, load_sem,
    normed, rms_s, hsend, hrecv, proj, unit, inv_s, ebuf,
    img, txt, igrad, tgrad, coef, town, beside,
    sib_send, sib_recv, zsend, zrecv, two_recv, yr1, yr2, xsend, xl_recv, xr_recv, ib_send, ib_recv,
    grad, dfull,
    local, c_send, c_recv, wy_send, wy_r1, wy_r2, wz_send, wz_recv, wc_send, wc_recv,
    h_sem, ix_sem, zr_sem, sb_sem, tx_sem, ty_sem, tf_sem,
    rsb_sem, rz_sem, two_sem, ry1_sem, ry2_sem, rx_sem, rr_sem, ib_sem, dx_sem,
    c_sem, wy1_sem, wy2_sem, wz_sem, wc_sem,
):
    dp = lax.axis_index("dp")
    tower = lax.axis_index("tower")
    mp = lax.axis_index("mp")
    x = tower * 2 + mp
    y = dp // 16
    z = (dp // 2) % 8
    c = dp % 2

    def at(nx, ny, nz, nc):
        return {"dp": (ny * NZ + nz) * 2 + nc, "tower": nx // 2, "mp": nx % 2}

    xl = at(tower * 2 + 1 - mp, y, z, c)
    xr = at(3 - x, y, z, c)
    sib = at(x, y, z, 1 - c)
    yn = (at(x, (y + 1) % NY, z, c), at(x, (y + NY - 1) % NY, z, c))
    zs = [at(x, y, (z + d) % NZ, c) for d in range(NZ)]
    zn = (zs[1], zs[NZ - 1])
    is_home = x >= 2
    is_image = x < 2
    first = jnp.where(is_home, x - 2, 1 - x)
    second = 1 - first
    order = (first, second)

    peers = [xl, xr, sib, yn[0], yn[1]] + zs[1:]
    barrier = pltpu.get_barrier_semaphore()
    for peer in peers:
        pl.semaphore_signal(barrier, inc=1, device_id=peer, device_id_type=MESH)

    load_pooled = pltpu.make_async_copy(pooled_in, pooled, load_sem.at[0])
    load_weight = pltpu.make_async_copy(weight_in, weight, load_sem.at[1])
    load_pooled.start()
    load_weight.start()

    sent = []
    mode = {"run": True, "keep": True}

    def copy(src, dst, sem, device):
        return pltpu.make_async_remote_copy(
            src_ref=src, dst_ref=dst, send_sem=sem.at[0], recv_sem=sem.at[1],
            device_id=device, device_id_type=MESH,
        )

    def send(src, dst, sem, device, cond=None):
        step = copy(src, dst, sem, device)
        if mode["run"]:
            step.start()
        if mode["keep"]:
            sent.append((cond, step))

    def send_if(cond, src, dst, sem, device):
        step = copy(src, dst, sem, device)
        pl.when(cond)(step.start)
        sent.append((cond, step))

    def arrived(dst, sem):
        if mode["run"]:
            copy(dst, dst, sem, sib).wait_recv()

    def settle(count):
        for cond, step in sent[:count]:
            if cond is None:
                step.wait_send()
            else:
                pl.when(cond)(step.wait_send)
        del sent[:count]

    def only(cond, work):
        mode["keep"] = False
        pl.when(cond)(work)
        mode["keep"] = True

    def keep(work):
        mode["run"] = False
        work()
        mode["run"] = True

    load_pooled.wait()
    full = pooled[0].astype(F32)
    rms = jnp.sqrt(jnp.mean(full * full, axis=-1, keepdims=True) + EPSILON)
    rms_s[...] = rms
    part = pooled[0, :, pl.ds(pl.multiple_of(mp * DH, DH), DH)].astype(F32)
    normed[...] = (part / rms).astype(BF16)
    theirs = pl.ds(pl.multiple_of((1 - mp) * OWN, OWN), OWN)
    mine = pl.ds(pl.multiple_of(mp * OWN, OWN), OWN)
    load_weight.wait()
    hsend[...] = dot(normed[theirs, :], weight[0], NT).astype(BF16).reshape(4, QUARTER, E)
    pl.semaphore_wait(barrier, len(peers))
    for j in TURN:
        send(hsend.at[j], hrecv.at[j], h_sem.at[j], xl)
    proj[...] = dot(normed[mine, :], weight[0], NT)

    def y_both(a, j):
        xs = order[a]
        for way, slot in ((0, 3), (1, 1)):
            send(txt.at[0, xs, j], txt.at[slot, xs, j], ty_sem.at[a, j, way], yn[way])

    def first_on(j):
        send(txt.at[0, first, j], txt.at[0, first, j], tx_sem.at[j, 1], xl)
        y_both(0, j)

    def own_image(ch):
        for way in (0, 1):
            to = POS[NZ - 1] if way == 0 else POS[1]
            send(img.at[0, 0, ch], img.at[to, 0, ch], zr_sem.at[0, way, ch], zn[way])
        send(img.at[0, 0, ch], img.at[0, 1, ch], sb_sem.at[0, ch], sib)

    for j in TURN:
        arrived(hrecv.at[j], h_sem.at[j])
        rows = pl.ds(j * QUARTER, QUARTER)
        value = proj[rows, :] + hrecv[j].astype(F32)
        inverse = lax.rsqrt(jnp.sum(value * value, axis=-1, keepdims=True) + EPSILON)
        inv_s[rows, :] = inverse
        unit_j = value * inverse
        unit[rows, :] = unit_j
        embedded = unit_j.astype(BF16)

        def text_start():
            send(txt.at[0, first, j], txt.at[0, first, j], tx_sem.at[j, 0], xr, is_home)
            first_on(j)

        def image_start():
            if j >= 2:
                send(ebuf.at[j - 2], img.at[0, 0, j - 2], ix_sem.at[j - 2], xr, is_image)
            else:
                own_image(j)

        def text_all():
            txt[0, first, j] = embedded
            text_start()

        def image_all():
            if j >= 2:
                ebuf[j - 2] = embedded
            else:
                img[0, 0, j] = embedded
            image_start()

        only(is_home, text_all)
        only(is_image, image_all)
        keep(text_start)
        keep(image_start)

    def ring(k, ch):
        for way in (0, 1):
            if k == 4 and ch != way:
                continue
            slot = (NZ - k) % NZ if way == 0 else k
            p = POS[slot]
            arrived(img.at[p, 0, ch], zr_sem.at[k - 1, way, ch])
            if k < 4 and not (k == 3 and ch != way):
                to = POS[(slot - 1) % NZ if way == 0 else (slot + 1) % NZ]
                send(img.at[p, 0, ch], img.at[to, 0, ch], zr_sem.at[k, way, ch], zn[way])
            send(img.at[p, 0, ch], img.at[p, 1, ch], sb_sem.at[p, ch], sib)

    def y_forward(a, j):
        xs = order[a]
        for way, slot in ((0, 3), (1, 1)):
            arrived(txt.at[slot, xs, j], ty_sem.at[a, j, way])
            if a == 0 and j // 2 == way:
                send(txt.at[slot, xs, j], txt.at[2, xs, j], tf_sem.at[0, j], yn[way])

    def two_away(j):
        arrived(txt.at[2, first, j], tf_sem.at[0, j])
        send(txt.at[2, first, j], txt.at[2, first, j], tf_sem.at[1, j], xl)

    def first_here(j):
        arrived(txt.at[0, first, j], tx_sem.at[j, 0])
        first_on(j)

    def second_on(j):
        arrived(txt.at[0, second, j], tx_sem.at[j, 1])
        y_both(1, j)

    def image_device():
        first_here(2)
        first_here(3)
        first_here(0)
        ring(1, 0)
        first_here(1)
        ring(1, 1)
        second_on(2)
        second_on(3)
        ring(2, 0)
        second_on(0)
        ring(2, 1)
        y_forward(0, 0)
        second_on(1)
        y_forward(0, 2)
        y_forward(0, 3)
        y_forward(0, 1)

    def text_device():
        for ch in (0, 1):
            arrived(img.at[0, 0, ch], ix_sem.at[ch])
            own_image(ch)
        both_devices()

    def both_devices():
        y_forward(0, 2)
        y_forward(0, 3)
        second_on(2)
        second_on(3)
        y_forward(0, 0)
        second_on(0)
        ring(1, 0)
        y_forward(0, 1)
        second_on(1)
        ring(1, 1)
        ring(2, 0)
        ring(2, 1)

    only(is_image, image_device)
    only(is_home, text_device)
    keep(both_devices)

    def sibling_images(low, high):
        for p in range(low, high):
            for ch in (0, 1):
                arrived(img.at[p, 1, ch], sb_sem.at[p, ch])

    mp_source = jnp.where(is_image, x, 3 - x)
    offset = jnp.where(is_image, 0, HALF)
    row = (pairs[pl.ds(mp_source, 1), :] - dp * ROWS).astype(F32)
    lane = lax.broadcasted_iota(jnp.int32, (HALF, OWN), 1)
    down = lax.broadcasted_iota(jnp.int32, (HALF, OWN), 0) + offset
    positions = jnp.sum(jnp.where(lane == down, row, 0.0), axis=1, keepdims=True)

    def block(t, low, high, masked=False):
        count = (high - low) * OWN
        images = img[low:high].reshape(count, E)
        texts = txt[t].reshape(ROWS, E)
        power = dot(images, texts, NT) * (-LOGIT_SCALE * LOG2E) - LOGIT_BIAS * LOG2E
        if masked:
            columns = lax.broadcasted_iota(jnp.int32, (HALF, ROWS), 1).astype(F32)
            sign = jnp.where(positions == columns, -1.0, 1.0)
            top = WEIGHT_PAIR * sign / (1.0 + jnp.exp2(jnp.minimum(sign * power[:HALF], MAX_POWER)))
            rest = WEIGHT_PAIR / (1.0 + jnp.exp2(jnp.minimum(power[HALF:], MAX_POWER)))
            coeffs = jnp.concatenate([top, rest], axis=0).astype(BF16)
        else:
            coeffs = (WEIGHT_PAIR / (1.0 + jnp.exp2(jnp.minimum(power, MAX_POWER)))).astype(BF16)
        coef[pl.ds(low * OWN, count), t * ROWS:(t + 1) * ROWS] = coeffs
        return dot(coeffs, images, TN)

    def image_block(low, high):
        rows = pl.ds(low * OWN, (high - low) * OWN)
        igrad[rows, :] = dot(coef[rows, :], txt[...].reshape(NY * ROWS, E))

    y_forward(1, 2)
    ring(3, 0)
    y_forward(1, 3)
    ring(3, 1)
    y_forward(1, 0)
    y_forward(1, 1)
    sibling_images(0, 5)
    town[...] = block(0, 0, 5, masked=True)
    two_away(2)
    two_away(3)
    ring(4, 0)
    beside[0] = block(1, 0, 5)
    two_away(0)
    two_away(1)
    ring(4, 1)
    beside[1] = block(3, 0, 5)
    sibling_images(5, 8)

    gathered = len(sent)

    for way, slot in ((0, 1), (1, 3)):
        tgrad[slot] = (beside[way] + block(slot, 5, 8)).astype(BF16).reshape(2, 4, QUARTER, E)
        for a, chunks in ((1, RTURN), (0, (2 - 2 * way, 3 - 2 * way))):
            for j in chunks:
                send(tgrad.at[slot, order[a], j], yr2.at[a, way, j], ry2_sem.at[a, way, j], yn[way])

    for j in range(4):
        arrived(txt.at[2, second, j], tf_sem.at[1, j])

    def sibling_rows(slot):
        p = POS[slot]
        sib_send[p] = igrad[pl.ds(p * OWN + HALF, HALF), :].astype(BF16)
        send(sib_send.at[p], sib_recv.at[p], rsb_sem.at[p], sib)

    def z_send(way, far, ch):
        slot = far if way == 0 else NZ - far
        p = POS[slot]
        rows = pl.ds(p * OWN + ch * QUARTER, QUARTER)
        value = igrad[rows, :] + sib_recv[p, pl.ds(ch * QUARTER, QUARTER), :].astype(F32)
        if far < 3 or (far == 3 and ch == way):
            arrived(zrecv.at[way, far, ch], rz_sem.at[way, far, ch])
            value = value + zrecv[way, far, ch].astype(F32)
        zsend[way, far - 1, ch] = value.astype(BF16)
        send(zsend.at[way, far - 1, ch], zrecv.at[way, far - 1, ch], rz_sem.at[way, far - 1, ch], zn[way])

    def sibling_here(*slots):
        for slot in slots:
            arrived(sib_recv.at[POS[slot]], rsb_sem.at[POS[slot]])

    tgrad[2] = block(2, 0, NZ).astype(BF16).reshape(2, 4, QUARTER, E)
    for j in RTURN:
        send(tgrad.at[2, second, j], two_recv.at[j], two_sem.at[j], xl)

    town[...] += block(0, 5, 8)
    image_block(5, 8)
    for slot in (4, 3, 5):
        sibling_rows(slot)
    image_block(3, 5)
    for slot in (2, 6):
        sibling_rows(slot)
    sibling_here(4, 3, 5)
    for way in (0, 1):
        z_send(way, 4, way)
    for way in (0, 1):
        z_send(way, 3, 1 - way)
    for j in RTURN:
        arrived(two_recv.at[j], two_sem.at[j])
        tgrad[2, first, j] = (tgrad[2, first, j].astype(F32) + two_recv[j].astype(F32)).astype(BF16)
        send(tgrad.at[2, first, j], yr1.at[j], ry1_sem.at[j], yn[j // 2])
    image_block(0, 3)
    for slot in (1, 7, 0):
        sibling_rows(slot)

    def y_second(i):
        for way, slot in ((0, 1), (1, 3)):
            j = 2 * way + i
            arrived(yr1.at[j], ry1_sem.at[j])
            tgrad[slot, first, j] = (tgrad[slot, first, j].astype(F32) + yr1[j].astype(F32)).astype(BF16)
            send(tgrad.at[slot, first, j], yr2.at[0, way, j], ry2_sem.at[0, way, j], yn[way])

    def z_next(far, other):
        for way in (0, 1):
            z_send(way, far, 1 - way if other else way)

    settle(gathered)
    def y_total(a, j):
        for way in (0, 1):
            arrived(yr2.at[a, way, j], ry2_sem.at[a, way, j])
        rows = pl.ds(pl.multiple_of(order[a] * OWN + j * QUARTER, QUARTER), QUARTER)
        return town[rows, :] + yr2[a, 0, j].astype(F32) + yr2[a, 1, j].astype(F32)

    def dx_copy(j):
        part = pl.ds(j * QUARTER, QUARTER)
        return copy(dfull.at[mp, part], dfull.at[mp, part], dx_sem.at[j], xl)

    def backward(j):
        part = pl.ds(j * QUARTER, QUARTER)
        unit_v = unit[part, :]
        grad_v = grad[part, :]
        dproj = (grad_v - unit_v * jnp.sum(unit_v * grad_v, axis=-1, keepdims=True)) * inv_s[part, :]
        dfull[mp, part] = dproj.astype(BF16)
        dx_copy(j).start()

    def second_sum(j):
        xsend[1, j] = y_total(1, j).astype(BF16)
        send(xsend.at[1, j], xl_recv.at[j], rx_sem.at[j], xl)

    def first_sum(j):
        value = y_total(0, j)
        arrived(xl_recv.at[j], rx_sem.at[j])
        return value + xl_recv[j].astype(F32)

    def image_sum(ch):
        rows = pl.ds(ch * QUARTER, QUARTER)
        value = igrad[rows, :] + sib_recv[0, rows, :].astype(F32)
        for way in (0, 1):
            arrived(zrecv.at[way, 0, ch], rz_sem.at[way, 0, ch])
            value = value + zrecv[way, 0, ch].astype(F32)
        return value

    def first_out(j):
        xsend[0, j] = first_sum(j).astype(BF16)
        send(xsend.at[0, j], xr_recv.at[j], rr_sem.at[j], xr, is_image)

    def image_out(ch):
        ib_send[ch] = image_sum(ch).astype(BF16)
        send(ib_send.at[ch], ib_recv.at[ch], ib_sem.at[ch], xr, is_home)

    z_next(3, False)
    second_sum(0)
    second_sum(2)
    sibling_here(2, 6, 1, 7, 0)
    z_next(2, True)
    second_sum(1)
    second_sum(3)
    y_second(0)
    z_next(2, False)
    y_second(1)
    z_next(1, True)
    z_next(1, False)

    def image_tail():
        first_out(0)
        first_out(2)
        for ch in (0, 1):
            grad[pl.ds(ch * QUARTER, QUARTER), :] = image_sum(ch)
            backward(ch)
        first_out(1)
        first_out(3)
        for ch in (0, 1):
            arrived(ib_recv.at[ch], ib_sem.at[ch])
            grad[pl.ds(HALF + ch * QUARTER, QUARTER), :] = ib_recv[ch].astype(F32)
            backward(2 + ch)

    def text_tail():
        grad[pl.ds(0, QUARTER), :] = first_sum(0)
        image_out(0)
        image_out(1)
        for j in (2, 1, 3):
            grad[pl.ds(j * QUARTER, QUARTER), :] = first_sum(j)
        for j in RTURN:
            arrived(xr_recv.at[j], rr_sem.at[j])
            rows = pl.ds(j * QUARTER, QUARTER)
            grad[rows, :] = grad[rows, :] + xr_recv[j].astype(F32)
            backward(j)

    only(is_image, image_tail)
    only(is_home, text_tail)
    for j in range(4):
        sent.append((is_image, copy(xsend.at[0, j], xr_recv.at[j], rr_sem.at[j], xr)))
    for ch in (0, 1):
        sent.append((is_home, copy(ib_send.at[ch], ib_recv.at[ch], ib_sem.at[ch], xr)))

    settle(len(sent) - 10)
    for j in range(4):
        sent.append((None, dx_copy(j)))
    for j in range(4):
        part = pl.ds(j * QUARTER, QUARTER)
        arrived(dfull.at[1 - mp, part], dx_sem.at[j])
    dproj_all = dfull[...].reshape(ROWS, E)

    theirs_l = pl.ds(pl.multiple_of((1 - c) * LANES, LANES), LANES)
    mine_l = pl.ds(pl.multiple_of(c * LANES, LANES), LANES)
    for l in range(3):
        local[l] = dot(dproj_all, normed[:, l * 2 * LANES:(l + 1) * 2 * LANES], TN)
        c_send[l] = local[l, :, theirs_l].astype(BF16)
        send(c_send.at[l], c_recv.at[l], c_sem.at[l], sib)

    dnormed = dot(dproj_all, weight[0])
    gin_out[0] = (dnormed / rms_s[...]).astype(BF16)

    settle(len(sent) - 3)
    EH = EY // 2

    def w_part(l, r, h):
        rows = pl.ds(pl.multiple_of(((y + r) % NY) * EY + h * EH, EH), EH)
        return local[l, rows, mine_l] + c_recv[l, rows, :].astype(F32)

    for l in range(3):
        arrived(c_recv.at[l], c_sem.at[l])
        for way in (0, 1):
            wy_send[l, way, 2] = w_part(l, 2, way).astype(BF16)
            send(wy_send.at[l, way, 2], wy_r1.at[l, way], wy1_sem.at[l, way], yn[way])
        for way, r in ((0, 1), (1, 3)):
            wy_send[l, way, 1 - way] = w_part(l, r, 1 - way).astype(BF16)
            send(wy_send.at[l, way, 1 - way], wy_r2.at[l, way, 1 - way], wy2_sem.at[l, way, 1 - way], yn[way])
    for l in range(3):
        for way, r in ((0, 1), (1, 3)):
            arrived(wy_r1.at[l, way], wy1_sem.at[l, way])
            wy_send[l, way, way] = (w_part(l, r, way) + wy_r1[l, way].astype(F32)).astype(BF16)
            send(wy_send.at[l, way, way], wy_r2.at[l, way, way], wy2_sem.at[l, way, way], yn[way])
    settle(len(sent) - 18)
    out_row = lax.broadcasted_iota(jnp.int32, (NZ * 48, EY), 0)
    in_row = lax.broadcasted_iota(jnp.int32, (NZ * 48, EY), 1)
    group = out_row // 24
    inner = out_row - group * 24
    spread = jnp.where(jnp.logical_and(inner < 18, in_row == group * 18 + inner), 1.0, 0.0).astype(BF16)
    for l in range(3):
        total = []
        for h in (0, 1):
            value = w_part(l, 0, h)
            for way in (0, 1):
                arrived(wy_r2.at[l, way, h], wy2_sem.at[l, way, h])
                value = value + wy_r2[l, way, h].astype(F32)
            total.append(value.astype(BF16))
        total = jnp.concatenate(total, axis=0)
        wz_send[l] = dot(spread, total).astype(BF16).reshape(NZ, 48, LANES)
        for d in (4, 3, 5, 2, 6, 1, 7):
            send(wz_send.at[l, (z + d) % NZ], wz_recv.at[l, d], wz_sem.at[l, d], zs[d])
    settle(len(sent) - 21)
    for l in range(3):
        value = wz_send[l, z].astype(F32)
        for d in range(1, NZ):
            arrived(wz_recv.at[l, d], wz_sem.at[l, d])
            value = value + wz_recv[l, d].astype(F32)
        wc_send[l] = value.reshape(2, 24, LANES)
        send(wc_send.at[l, 1 - c], wc_recv.at[l], wc_sem.at[l], sib)
        gw_out[0, :, pl.ds(pl.multiple_of((2 * l + c) * LANES, LANES), LANES)] = wc_send[l, c, :18, :]
    for l in range(3):
        arrived(wc_recv.at[l], wc_sem.at[l])
        gw_out[0, :, pl.ds(pl.multiple_of((2 * l + 1 - c) * LANES, LANES), LANES)] = wc_recv[l, :18, :]

    settle(len(sent))


def finish(head, pooled, head_out, pooled_out):
    head_out[:, 0, :] = head[0]
    pooled_out[...] = pooled[...]


def scratch():
    vmem, dma = pltpu.VMEM, pltpu.SemaphoreType.DMA
    return [
        vmem((1, ROWS, D), BF16), vmem((1, E, DH), BF16), dma((2,)),
        vmem((ROWS, DH), BF16), vmem((ROWS, 1), F32), vmem((4, QUARTER, E), BF16), vmem((4, QUARTER, E), BF16),
        vmem((OWN, E), F32), vmem((OWN, E), F32), vmem((OWN, 1), F32), vmem((2, QUARTER, E), BF16),
        vmem((NZ, 2, 2, QUARTER, E), BF16), vmem((NY, 2, 4, QUARTER, E), BF16),
        vmem((NZ * OWN, E), F32), vmem((NY, 2, 4, QUARTER, E), BF16), vmem((NZ * OWN, NY * ROWS), BF16), vmem((ROWS, E), F32), vmem((2, ROWS, E), F32),
        vmem((NZ, HALF, E), BF16), vmem((NZ, HALF, E), BF16),
        vmem((2, 4, 2, QUARTER, E), BF16), vmem((2, 4, 2, QUARTER, E), BF16),
        vmem((4, QUARTER, E), BF16), vmem((4, QUARTER, E), BF16), vmem((2, 2, 4, QUARTER, E), BF16),
        vmem((2, 4, QUARTER, E), BF16), vmem((4, QUARTER, E), BF16), vmem((4, QUARTER, E), BF16),
        vmem((2, QUARTER, E), BF16), vmem((2, QUARTER, E), BF16),
        vmem((OWN, E), F32), vmem((2, OWN, E), BF16),
        vmem((3, E, 2 * LANES), F32), vmem((3, E, LANES), BF16), vmem((3, E, LANES), BF16),
        vmem((3, 2, 3, EY // 2, LANES), BF16), vmem((3, 2, EY // 2, LANES), BF16), vmem((3, 2, 2, EY // 2, LANES), BF16),
        vmem((3, NZ, 48, LANES), BF16), vmem((3, NZ, 48, LANES), BF16),
        vmem((3, 2, 24, LANES), F32), vmem((3, 24, LANES), F32),
        dma((4, 2)), dma((2, 2)), dma((4, 2, 2, 2)), dma((NZ, 2, 2)), dma((4, 2, 2)), dma((2, 4, 2, 2)),
        dma((2, 4, 2)),
        dma((NZ, 2)), dma((2, 4, 2, 2)), dma((4, 2)), dma((4, 2)), dma((2, 2, 4, 2)), dma((4, 2)), dma((4, 2)),
        dma((2, 2)), dma((4, 2)),
        dma((3, 2)), dma((3, 2, 2)), dma((3, 2, 2, 2)), dma((3, NZ, 2)), dma((3, 2)),
    ]


def shards(inputs, head_weight, pair_index):
    space = pl.BlockSpec(memory_space=pltpu.VMEM)
    grads = pl.pallas_call(
        kernel,
        out_shape=(
            jax.ShapeDtypeStruct((1, E // 64, DH), F32),
            jax.ShapeDtypeStruct((1, ROWS, DH), BF16),
        ),
        in_specs=[pl.BlockSpec(memory_space=pl.ANY)] * 2 + [space],
        out_specs=(space, space),
        scratch_shapes=scratch(),
        compiler_params=pltpu.CompilerParams(
            collective_id=0, has_side_effects=True, vmem_limit_bytes=60 * 2**20
        ),
    )(inputs, head_weight, pair_index.reshape(2, OWN))
    head, pooled = pl.pallas_call(
        finish,
        out_shape=(
            jax.ShapeDtypeStruct((E // 64, 1, DH), F32),
            jax.ShapeDtypeStruct((1, ROWS, DH), BF16),
        ),
        in_specs=[space] * 2,
        out_specs=(space, space),
    )(*grads)
    return head.reshape(1, E // 64, DH), pooled


def solution(mesh):
    in_specs = (P("tower", "dp", None), P("tower", None, "mp"), P("dp"))
    out_specs = (P("tower", "dp", "mp"), P("tower", "dp", "mp"))
    return jax.shard_map(shards, mesh=mesh, in_specs=in_specs, out_specs=out_specs, check_vma=False)
```

```python
import jax
import jax.numpy as jnp
from jax import lax
from jax.experimental import pallas as pl
from jax.experimental.pallas import tpu as pltpu
from jax.sharding import PartitionSpec as P

EPSILON = 1e-06
LOGIT_SCALE = 100.0
LOGIT_BIAS = -10.0
BATCH = 16384
LOSS_SCALE = 16384.0
WEIGHT_PAIR = LOSS_SCALE * LOGIT_SCALE / BATCH
LOG2E = 1.4426950408889634
MAX_POWER = 126.0
NX, NY, NZ = 4, 4, 8
ROWS = 256
OWN = 128
HALF = 64
QUARTER = 32
E = 1152
D = 1536
DH = 768
LANES = 128
POS = (0, 1, 3, 5, 7, 6, 4, 2)
EY = 288
TURN = (2, 3, 0, 1)
RTURN = (0, 2, 1, 3)
F32 = jnp.float32
BF16 = jnp.bfloat16
MESH = pl.DeviceIdType.MESH
NT = (((1,), (1,)), ((), ()))
TN = (((0,), (0,)), ((), ()))


def dot(a, b, dims=(((1,), (0,)), ((), ()))):
    return lax.dot_general(a, b, dims, preferred_element_type=F32)


def kernel(
    pooled_in, weight_in, pairs, gw_out, gin_out,
    pooled, weight, gin, load_sem,
    normed, rms_s, hsend, hrecv, proj, unit, inv_s, ebuf,
    img, txt, igrad, tgrad, coef, town, beside,
    sib_send, sib_recv, zsend, zrecv, two_recv, yr1, yr2, xsend, xl_recv, xr_recv, ib_send, ib_recv,
    grad, dfull,
    local, c_send, c_recv, wy_send, wy_r1, wy_r2, wz_send, wz_recv, wc_send, wc_recv,
    h_sem, ix_sem, zr_sem, sb_sem, tx_sem, ty_sem, tf_sem,
    rsb_sem, rz_sem, two_sem, ry1_sem, ry2_sem, rx_sem, rr_sem, ib_sem, dx_sem,
    c_sem, wy1_sem, wy2_sem, wz_sem, wc_sem,
):
    dp = lax.axis_index("dp")
    tower = lax.axis_index("tower")
    mp = lax.axis_index("mp")
    x = tower * 2 + mp
    y = dp // 16
    z = (dp // 2) % 8
    c = dp % 2

    def at(nx, ny, nz, nc):
        return {"dp": (ny * NZ + nz) * 2 + nc, "tower": nx // 2, "mp": nx % 2}

    xl = at(tower * 2 + 1 - mp, y, z, c)
    xr = at(3 - x, y, z, c)
    sib = at(x, y, z, 1 - c)
    yn = (at(x, (y + 1) % NY, z, c), at(x, (y + NY - 1) % NY, z, c))
    zs = [at(x, y, (z + d) % NZ, c) for d in range(NZ)]
    zn = (zs[1], zs[NZ - 1])
    is_home = x >= 2
    is_image = x < 2
    first = jnp.where(is_home, x - 2, 1 - x)
    second = 1 - first
    order = (first, second)

    peers = [xl, xr, sib, yn[0], yn[1]] + zs[1:]
    barrier = pltpu.get_barrier_semaphore()
    for peer in peers:
        pl.semaphore_signal(barrier, inc=1, device_id=peer, device_id_type=MESH)

    load_pooled = pltpu.make_async_copy(pooled_in, pooled, load_sem.at[0])
    load_weight = pltpu.make_async_copy(weight_in, weight, load_sem.at[1])
    load_pooled.start()
    load_weight.start()

    sent = []
    mode = {"run": True, "keep": True}

    def copy(src, dst, sem, device):
        return pltpu.make_async_remote_copy(
            src_ref=src, dst_ref=dst, send_sem=sem.at[0], recv_sem=sem.at[1],
            device_id=device, device_id_type=MESH,
        )

    def send(src, dst, sem, device, cond=None):
        step = copy(src, dst, sem, device)
        if mode["run"]:
            step.start()
        if mode["keep"]:
            sent.append((cond, step))

    def send_if(cond, src, dst, sem, device):
        step = copy(src, dst, sem, device)
        pl.when(cond)(step.start)
        sent.append((cond, step))

    def arrived(dst, sem):
        if mode["run"]:
            copy(dst, dst, sem, sib).wait_recv()

    def settle(count):
        for cond, step in sent[:count]:
            if cond is None:
                step.wait_send()
            else:
                pl.when(cond)(step.wait_send)
        del sent[:count]

    def only(cond, work):
        mode["keep"] = False
        pl.when(cond)(work)
        mode["keep"] = True

    def keep(work):
        mode["run"] = False
        work()
        mode["run"] = True

    load_pooled.wait()
    full = pooled[0].astype(F32)
    rms = jnp.sqrt(jnp.mean(full * full, axis=-1, keepdims=True) + EPSILON)
    rms_s[...] = rms
    part = pooled[0, :, pl.ds(pl.multiple_of(mp * DH, DH), DH)].astype(F32)
    normed[...] = (part / rms).astype(BF16)
    theirs = pl.ds(pl.multiple_of((1 - mp) * OWN, OWN), OWN)
    mine = pl.ds(pl.multiple_of(mp * OWN, OWN), OWN)
    load_weight.wait()
    hsend[...] = dot(normed[theirs, :], weight[0], NT).astype(BF16).reshape(4, QUARTER, E)
    pl.semaphore_wait(barrier, len(peers))
    for j in TURN:
        send(hsend.at[j], hrecv.at[j], h_sem.at[j], xl)
    proj[...] = dot(normed[mine, :], weight[0], NT)

    def y_both(a, j):
        xs = order[a]
        for way, slot in ((0, 3), (1, 1)):
            send(txt.at[0, xs, j], txt.at[slot, xs, j], ty_sem.at[a, j, way], yn[way])

    def first_on(j):
        send(txt.at[0, first, j], txt.at[0, first, j], tx_sem.at[j, 1], xl)
        y_both(0, j)

    def own_image(ch):
        for way in (0, 1):
            to = POS[NZ - 1] if way == 0 else POS[1]
            send(img.at[0, 0, ch], img.at[to, 0, ch], zr_sem.at[0, way, ch], zn[way])
        send(img.at[0, 0, ch], img.at[0, 1, ch], sb_sem.at[0, ch], sib)

    for j in TURN:
        arrived(hrecv.at[j], h_sem.at[j])
        rows = pl.ds(j * QUARTER, QUARTER)
        value = proj[rows, :] + hrecv[j].astype(F32)
        inverse = lax.rsqrt(jnp.sum(value * value, axis=-1, keepdims=True) + EPSILON)
        inv_s[rows, :] = inverse
        unit_j = value * inverse
        unit[rows, :] = unit_j
        embedded = unit_j.astype(BF16)

        def text_start():
            send(txt.at[0, first, j], txt.at[0, first, j], tx_sem.at[j, 0], xr, is_home)
            first_on(j)

        def image_start():
            if j >= 2:
                send(ebuf.at[j - 2], img.at[0, 0, j - 2], ix_sem.at[j - 2], xr, is_image)
            else:
                own_image(j)

        def text_all():
            txt[0, first, j] = embedded
            text_start()

        def image_all():
            if j >= 2:
                ebuf[j - 2] = embedded
            else:
                img[0, 0, j] = embedded
            image_start()

        only(is_home, text_all)
        only(is_image, image_all)
        keep(text_start)
        keep(image_start)

    def ring(k, ch):
        for way in (0, 1):
            if k == 4 and ch != way:
                continue
            slot = (NZ - k) % NZ if way == 0 else k
            p = POS[slot]
            arrived(img.at[p, 0, ch], zr_sem.at[k - 1, way, ch])
            if k < 4 and not (k == 3 and ch != way):
                to = POS[(slot - 1) % NZ if way == 0 else (slot + 1) % NZ]
                send(img.at[p, 0, ch], img.at[to, 0, ch], zr_sem.at[k, way, ch], zn[way])
            send(img.at[p, 0, ch], img.at[p, 1, ch], sb_sem.at[p, ch], sib)

    def y_forward(a, j):
        xs = order[a]
        for way, slot in ((0, 3), (1, 1)):
            arrived(txt.at[slot, xs, j], ty_sem.at[a, j, way])
            if a == 0 and j // 2 == way:
                send(txt.at[slot, xs, j], txt.at[2, xs, j], tf_sem.at[0, j], yn[way])

    def two_away(j):
        arrived(txt.at[2, first, j], tf_sem.at[0, j])
        send(txt.at[2, first, j], txt.at[2, first, j], tf_sem.at[1, j], xl)

    def first_here(j):
        arrived(txt.at[0, first, j], tx_sem.at[j, 0])
        first_on(j)

    def second_on(j):
        arrived(txt.at[0, second, j], tx_sem.at[j, 1])
        y_both(1, j)

    def image_device():
        first_here(2)
        first_here(3)
        first_here(0)
        ring(1, 0)
        first_here(1)
        ring(1, 1)
        second_on(2)
        second_on(3)
        ring(2, 0)
        second_on(0)
        ring(2, 1)
        y_forward(0, 0)
        second_on(1)
        y_forward(0, 2)
        y_forward(0, 3)
        y_forward(0, 1)

    def text_device():
        for ch in (0, 1):
            arrived(img.at[0, 0, ch], ix_sem.at[ch])
            own_image(ch)
        both_devices()

    def both_devices():
        y_forward(0, 2)
        y_forward(0, 3)
        second_on(2)
        second_on(3)
        y_forward(0, 0)
        second_on(0)
        ring(1, 0)
        y_forward(0, 1)
        second_on(1)
        ring(1, 1)
        ring(2, 0)
        ring(2, 1)

    only(is_image, image_device)
    only(is_home, text_device)
    keep(both_devices)

    def sibling_images(low, high):
        for p in range(low, high):
            for ch in (0, 1):
                arrived(img.at[p, 1, ch], sb_sem.at[p, ch])

    mp_source = jnp.where(is_image, x, 3 - x)
    offset = jnp.where(is_image, 0, HALF)
    row = (pairs[pl.ds(mp_source, 1), :] - dp * ROWS).astype(F32)
    lane = lax.broadcasted_iota(jnp.int32, (HALF, OWN), 1)
    down = lax.broadcasted_iota(jnp.int32, (HALF, OWN), 0) + offset
    positions = jnp.sum(jnp.where(lane == down, row, 0.0), axis=1, keepdims=True)

    def block(t, low, high, masked=False):
        count = (high - low) * OWN
        images = img[low:high].reshape(count, E)
        texts = txt[t].reshape(ROWS, E)
        power = dot(images, texts, NT) * (-LOGIT_SCALE * LOG2E) - LOGIT_BIAS * LOG2E
        if masked:
            columns = lax.broadcasted_iota(jnp.int32, (HALF, ROWS), 1).astype(F32)
            sign = jnp.where(positions == columns, -1.0, 1.0)
            top = WEIGHT_PAIR * sign / (1.0 + jnp.exp2(jnp.minimum(sign * power[:HALF], MAX_POWER)))
            rest = WEIGHT_PAIR / (1.0 + jnp.exp2(jnp.minimum(power[HALF:], MAX_POWER)))
            coeffs = jnp.concatenate([top, rest], axis=0).astype(BF16)
        else:
            coeffs = (WEIGHT_PAIR / (1.0 + jnp.exp2(jnp.minimum(power, MAX_POWER)))).astype(BF16)
        coef[pl.ds(low * OWN, count), t * ROWS:(t + 1) * ROWS] = coeffs
        return dot(coeffs, images, TN)

    def image_block(low, high):
        rows = pl.ds(low * OWN, (high - low) * OWN)
        igrad[rows, :] = dot(coef[rows, :], txt[...].reshape(NY * ROWS, E))

    y_forward(1, 2)
    ring(3, 0)
    y_forward(1, 3)
    ring(3, 1)
    y_forward(1, 0)
    y_forward(1, 1)
    sibling_images(0, 5)
    town[...] = block(0, 0, 5, masked=True)
    two_away(2)
    two_away(3)
    ring(4, 0)
    beside[0] = block(1, 0, 5)
    two_away(0)
    two_away(1)
    ring(4, 1)
    beside[1] = block(3, 0, 5)
    sibling_images(5, 8)

    gathered = len(sent)

    for way, slot in ((0, 1), (1, 3)):
        tgrad[slot] = (beside[way] + block(slot, 5, 8)).astype(BF16).reshape(2, 4, QUARTER, E)
        for a, chunks in ((1, RTURN), (0, (2 - 2 * way, 3 - 2 * way))):
            for j in chunks:
                send(tgrad.at[slot, order[a], j], yr2.at[a, way, j], ry2_sem.at[a, way, j], yn[way])

    for j in range(4):
        arrived(txt.at[2, second, j], tf_sem.at[1, j])

    def sibling_rows(slot):
        p = POS[slot]
        sib_send[p] = igrad[pl.ds(p * OWN + HALF, HALF), :].astype(BF16)
        send(sib_send.at[p], sib_recv.at[p], rsb_sem.at[p], sib)

    def z_send(way, far, ch):
        slot = far if way == 0 else NZ - far
        p = POS[slot]
        rows = pl.ds(p * OWN + ch * QUARTER, QUARTER)
        value = igrad[rows, :] + sib_recv[p, pl.ds(ch * QUARTER, QUARTER), :].astype(F32)
        if far < 3 or (far == 3 and ch == way):
            arrived(zrecv.at[way, far, ch], rz_sem.at[way, far, ch])
            value = value + zrecv[way, far, ch].astype(F32)
        zsend[way, far - 1, ch] = value.astype(BF16)
        send(zsend.at[way, far - 1, ch], zrecv.at[way, far - 1, ch], rz_sem.at[way, far - 1, ch], zn[way])

    def sibling_here(*slots):
        for slot in slots:
            arrived(sib_recv.at[POS[slot]], rsb_sem.at[POS[slot]])

    tgrad[2] = block(2, 0, NZ).astype(BF16).reshape(2, 4, QUARTER, E)
    for j in RTURN:
        send(tgrad.at[2, second, j], two_recv.at[j], two_sem.at[j], xl)

    town[...] += block(0, 5, 8)
    image_block(5, 8)
    for slot in (4, 3, 5):
        sibling_rows(slot)
    image_block(3, 5)
    for slot in (2, 6):
        sibling_rows(slot)
    sibling_here(4, 3, 5)
    for way in (0, 1):
        z_send(way, 4, way)
    for way in (0, 1):
        z_send(way, 3, 1 - way)
    for j in RTURN:
        arrived(two_recv.at[j], two_sem.at[j])
        tgrad[2, first, j] = (tgrad[2, first, j].astype(F32) + two_recv[j].astype(F32)).astype(BF16)
        send(tgrad.at[2, first, j], yr1.at[j], ry1_sem.at[j], yn[j // 2])
    image_block(0, 3)
    for slot in (1, 7, 0):
        sibling_rows(slot)

    def y_second(i):
        for way, slot in ((0, 1), (1, 3)):
            j = 2 * way + i
            arrived(yr1.at[j], ry1_sem.at[j])
            tgrad[slot, first, j] = (tgrad[slot, first, j].astype(F32) + yr1[j].astype(F32)).astype(BF16)
            send(tgrad.at[slot, first, j], yr2.at[0, way, j], ry2_sem.at[0, way, j], yn[way])

    def z_next(far, other):
        for way in (0, 1):
            z_send(way, far, 1 - way if other else way)

    settle(gathered)
    def y_total(a, j):
        for way in (0, 1):
            arrived(yr2.at[a, way, j], ry2_sem.at[a, way, j])
        rows = pl.ds(pl.multiple_of(order[a] * OWN + j * QUARTER, QUARTER), QUARTER)
        return town[rows, :] + yr2[a, 0, j].astype(F32) + yr2[a, 1, j].astype(F32)

    def dx_copy(j):
        part = pl.ds(j * QUARTER, QUARTER)
        return copy(dfull.at[mp, part], dfull.at[mp, part], dx_sem.at[j], xl)

    def backward(j):
        part = pl.ds(j * QUARTER, QUARTER)
        unit_v = unit[part, :]
        grad_v = grad[part, :]
        dproj = (grad_v - unit_v * jnp.sum(unit_v * grad_v, axis=-1, keepdims=True)) * inv_s[part, :]
        dfull[mp, part] = dproj.astype(BF16)
        dx_copy(j).start()

    def second_sum(j):
        xsend[1, j] = y_total(1, j).astype(BF16)
        send(xsend.at[1, j], xl_recv.at[j], rx_sem.at[j], xl)

    def first_sum(j):
        value = y_total(0, j)
        arrived(xl_recv.at[j], rx_sem.at[j])
        return value + xl_recv[j].astype(F32)

    def image_sum(ch):
        rows = pl.ds(ch * QUARTER, QUARTER)
        value = igrad[rows, :] + sib_recv[0, rows, :].astype(F32)
        for way in (0, 1):
            arrived(zrecv.at[way, 0, ch], rz_sem.at[way, 0, ch])
            value = value + zrecv[way, 0, ch].astype(F32)
        return value

    def first_out(j):
        xsend[0, j] = first_sum(j).astype(BF16)
        send(xsend.at[0, j], xr_recv.at[j], rr_sem.at[j], xr, is_image)

    def image_out(ch):
        ib_send[ch] = image_sum(ch).astype(BF16)
        send(ib_send.at[ch], ib_recv.at[ch], ib_sem.at[ch], xr, is_home)

    z_next(3, False)
    second_sum(0)
    second_sum(2)
    sibling_here(2, 6, 1, 7, 0)
    z_next(2, True)
    second_sum(1)
    second_sum(3)
    y_second(0)
    z_next(2, False)
    y_second(1)
    z_next(1, True)
    z_next(1, False)

    def image_tail():
        first_out(0)
        first_out(2)
        for ch in (0, 1):
            grad[pl.ds(ch * QUARTER, QUARTER), :] = image_sum(ch)
            backward(ch)
        first_out(1)
        first_out(3)
        for ch in (0, 1):
            arrived(ib_recv.at[ch], ib_sem.at[ch])
            grad[pl.ds(HALF + ch * QUARTER, QUARTER), :] = ib_recv[ch].astype(F32)
            backward(2 + ch)

    def text_tail():
        grad[pl.ds(0, QUARTER), :] = first_sum(0)
        image_out(0)
        image_out(1)
        for j in (2, 1, 3):
            grad[pl.ds(j * QUARTER, QUARTER), :] = first_sum(j)
        for j in RTURN:
            arrived(xr_recv.at[j], rr_sem.at[j])
            rows = pl.ds(j * QUARTER, QUARTER)
            grad[rows, :] = grad[rows, :] + xr_recv[j].astype(F32)
            backward(j)

    only(is_image, image_tail)
    only(is_home, text_tail)
    for j in range(4):
        sent.append((is_image, copy(xsend.at[0, j], xr_recv.at[j], rr_sem.at[j], xr)))
    for ch in (0, 1):
        sent.append((is_home, copy(ib_send.at[ch], ib_recv.at[ch], ib_sem.at[ch], xr)))

    settle(len(sent) - 10)
    for j in range(4):
        sent.append((None, dx_copy(j)))
    for j in range(4):
        part = pl.ds(j * QUARTER, QUARTER)
        arrived(dfull.at[1 - mp, part], dx_sem.at[j])
    dproj_all = dfull[...].reshape(ROWS, E)

    theirs_l = pl.ds(pl.multiple_of((1 - c) * LANES, LANES), LANES)
    mine_l = pl.ds(pl.multiple_of(c * LANES, LANES), LANES)
    for l in range(3):
        local[l] = dot(dproj_all, normed[:, l * 2 * LANES:(l + 1) * 2 * LANES], TN)
        c_send[l] = local[l, :, theirs_l].astype(BF16)
        send(c_send.at[l], c_recv.at[l], c_sem.at[l], sib)

    dnormed = dot(dproj_all, weight[0])
    gin[0] = (dnormed / rms_s[...]).astype(BF16)
    store_gin = pltpu.make_async_copy(gin, gin_out, load_sem.at[2])
    store_gin.start()

    settle(len(sent) - 3)
    EH = EY // 2

    def w_part(l, r, h):
        rows = pl.ds(pl.multiple_of(((y + r) % NY) * EY + h * EH, EH), EH)
        return local[l, rows, mine_l] + c_recv[l, rows, :].astype(F32)

    for l in range(3):
        arrived(c_recv.at[l], c_sem.at[l])
        for way in (0, 1):
            wy_send[l, way, 2] = w_part(l, 2, way).astype(BF16)
            send(wy_send.at[l, way, 2], wy_r1.at[l, way], wy1_sem.at[l, way], yn[way])
        for way, r in ((0, 1), (1, 3)):
            wy_send[l, way, 1 - way] = w_part(l, r, 1 - way).astype(BF16)
            send(wy_send.at[l, way, 1 - way], wy_r2.at[l, way, 1 - way], wy2_sem.at[l, way, 1 - way], yn[way])
    for l in range(3):
        for way, r in ((0, 1), (1, 3)):
            arrived(wy_r1.at[l, way], wy1_sem.at[l, way])
            wy_send[l, way, way] = (w_part(l, r, way) + wy_r1[l, way].astype(F32)).astype(BF16)
            send(wy_send.at[l, way, way], wy_r2.at[l, way, way], wy2_sem.at[l, way, way], yn[way])
    settle(len(sent) - 18)
    out_row = lax.broadcasted_iota(jnp.int32, (NZ * 48, EY), 0)
    in_row = lax.broadcasted_iota(jnp.int32, (NZ * 48, EY), 1)
    group = out_row // 24
    inner = out_row - group * 24
    spread = jnp.where(jnp.logical_and(inner < 18, in_row == group * 18 + inner), 1.0, 0.0).astype(BF16)
    for l in range(3):
        total = []
        for h in (0, 1):
            value = w_part(l, 0, h)
            for way in (0, 1):
                arrived(wy_r2.at[l, way, h], wy2_sem.at[l, way, h])
                value = value + wy_r2[l, way, h].astype(F32)
            total.append(value.astype(BF16))
        total = jnp.concatenate(total, axis=0)
        wz_send[l] = dot(spread, total).astype(BF16).reshape(NZ, 48, LANES)
        for d in (4, 3, 5, 2, 6, 1, 7):
            send(wz_send.at[l, (z + d) % NZ], wz_recv.at[l, d], wz_sem.at[l, d], zs[d])
    settle(len(sent) - 21)
    for l in range(3):
        value = wz_send[l, z].astype(F32)
        for d in range(1, NZ):
            arrived(wz_recv.at[l, d], wz_sem.at[l, d])
            value = value + wz_recv[l, d].astype(F32)
        wc_send[l] = value.reshape(2, 24, LANES)
        send(wc_send.at[l, 1 - c], wc_recv.at[l], wc_sem.at[l], sib)
        gw_out[0, :, pl.ds(pl.multiple_of((2 * l + c) * LANES, LANES), LANES)] = wc_send[l, c, :18, :]
    for l in range(3):
        arrived(wc_recv.at[l], wc_sem.at[l])
        gw_out[0, :, pl.ds(pl.multiple_of((2 * l + 1 - c) * LANES, LANES), LANES)] = wc_recv[l, :18, :]

    store_gin.wait()
    settle(len(sent))


def finish(head, pooled, head_out, pooled_out, sem):
    step = pltpu.make_async_copy(pooled, pooled_out, sem)
    step.start()
    head_out[:, 0, :] = head[0]
    step.wait()


def scratch():
    vmem, dma = pltpu.VMEM, pltpu.SemaphoreType.DMA
    return [
        vmem((1, ROWS, D), BF16), vmem((1, E, DH), BF16), vmem((1, ROWS, DH), BF16), dma((3,)),
        vmem((ROWS, DH), BF16), vmem((ROWS, 1), F32), vmem((4, QUARTER, E), BF16), vmem((4, QUARTER, E), BF16),
        vmem((OWN, E), F32), vmem((OWN, E), F32), vmem((OWN, 1), F32), vmem((2, QUARTER, E), BF16),
        vmem((NZ, 2, 2, QUARTER, E), BF16), vmem((NY, 2, 4, QUARTER, E), BF16),
        vmem((NZ * OWN, E), F32), vmem((NY, 2, 4, QUARTER, E), BF16), vmem((NZ * OWN, NY * ROWS), BF16), vmem((ROWS, E), F32), vmem((2, ROWS, E), F32),
        vmem((NZ, HALF, E), BF16), vmem((NZ, HALF, E), BF16),
        vmem((2, 4, 2, QUARTER, E), BF16), vmem((2, 4, 2, QUARTER, E), BF16),
        vmem((4, QUARTER, E), BF16), vmem((4, QUARTER, E), BF16), vmem((2, 2, 4, QUARTER, E), BF16),
        vmem((2, 4, QUARTER, E), BF16), vmem((4, QUARTER, E), BF16), vmem((4, QUARTER, E), BF16),
        vmem((2, QUARTER, E), BF16), vmem((2, QUARTER, E), BF16),
        vmem((OWN, E), F32), vmem((2, OWN, E), BF16),
        vmem((3, E, 2 * LANES), F32), vmem((3, E, LANES), BF16), vmem((3, E, LANES), BF16),
        vmem((3, 2, 3, EY // 2, LANES), BF16), vmem((3, 2, EY // 2, LANES), BF16), vmem((3, 2, 2, EY // 2, LANES), BF16),
        vmem((3, NZ, 48, LANES), BF16), vmem((3, NZ, 48, LANES), BF16),
        vmem((3, 2, 24, LANES), F32), vmem((3, 24, LANES), F32),
        dma((4, 2)), dma((2, 2)), dma((4, 2, 2, 2)), dma((NZ, 2, 2)), dma((4, 2, 2)), dma((2, 4, 2, 2)),
        dma((2, 4, 2)),
        dma((NZ, 2)), dma((2, 4, 2, 2)), dma((4, 2)), dma((4, 2)), dma((2, 2, 4, 2)), dma((4, 2)), dma((4, 2)),
        dma((2, 2)), dma((4, 2)),
        dma((3, 2)), dma((3, 2, 2)), dma((3, 2, 2, 2)), dma((3, NZ, 2)), dma((3, 2)),
    ]


def shards(inputs, head_weight, pair_index):
    space = pl.BlockSpec(memory_space=pltpu.VMEM)
    grads = pl.pallas_call(
        kernel,
        out_shape=(
            jax.ShapeDtypeStruct((1, E // 64, DH), F32),
            jax.ShapeDtypeStruct((1, ROWS, DH), BF16),
        ),
        in_specs=[pl.BlockSpec(memory_space=pl.ANY)] * 2 + [space],
        out_specs=(space, pl.BlockSpec(memory_space=pl.ANY)),
        scratch_shapes=scratch(),
        compiler_params=pltpu.CompilerParams(
            collective_id=0, has_side_effects=True, vmem_limit_bytes=60 * 2**20
        ),
    )(inputs, head_weight, pair_index.reshape(2, OWN))
    head, pooled = pl.pallas_call(
        finish,
        out_shape=(
            jax.ShapeDtypeStruct((E // 64, 1, DH), F32),
            jax.ShapeDtypeStruct((1, ROWS, DH), BF16),
        ),
        in_specs=[space, pl.BlockSpec(memory_space=pl.ANY)],
        out_specs=(space, pl.BlockSpec(memory_space=pl.ANY)),
        scratch_shapes=[pltpu.SemaphoreType.DMA],
    )(*grads)
    return head.reshape(1, E // 64, DH), pooled


def solution(mesh):
    in_specs = (P("tower", "dp", None), P("tower", None, "mp"), P("dp"))
    out_specs = (P("tower", "dp", "mp"), P("tower", "dp", "mp"))
    return jax.shard_map(shards, mesh=mesh, in_specs=in_specs, out_specs=out_specs, check_vma=False)
```
